128 devices in a mesh: seq: 16 (over z_lo, y, core), ch: 8 (over x, z_hi).
Axes of the slice: x: 4, y: 4, z: 4 (z_hi: 2, z_lo: 2; z = z_hi * 2 + z_lo), core: 2. Of those that a mesh axis runs over, the one named last changes fastest.
Arguments:
- inputs: bfloat16 [65536, 1536], P('seq', 'ch'), may hold values from -6 to 6
- factor_one: bfloat16 [256, 256, 256], P('seq'), may hold values from -0.375 to 0.375
- factor_two: bfloat16 [256, 256, 256], P('seq'), may hold values from -0.375 to 0.375
- w_input_gate: bfloat16 [1536, 384], P(('seq', 'ch')), may hold values from -0.3125 to 0.3125
- norm_gain: float32 [1536], replicated, may hold values from 0.25 to 1.75
- w_gate: bfloat16 [1536, 768], P(('seq', 'ch')), may hold values from -0.3125 to 0.3125
- w_up: bfloat16 [1536, 768], P(('seq', 'ch')), may hold values from -0.3125 to 0.3125
- w_down: bfloat16 [3072, 384], P(('seq', 'ch')), may hold values from -0.21875 to 0.21875
- grad_out: bfloat16 [65536, 1536], P(('seq', 'ch')), may hold values from -6 to 6
Outputs:
- mixed_out: bfloat16 [65536, 1536], P(('seq', 'ch'))
- grad_inputs: bfloat16 [65536, 1536], P('seq', 'ch')
- grad_factor_one: float32 [256, 256, 256], P('seq', 'ch')
- grad_factor_two: float32 [256, 256, 256], P('seq', 'ch')
- grad_w_input_gate: float32 [1536, 384], P(('seq', 'ch'))
- grad_norm_gain: float32 [1536], replicated
- grad_w_gate: float32 [1536, 768], P(('seq', 'ch'))
- grad_w_up: float32 [1536, 768], P(('seq', 'ch'))
- grad_w_down: float32 [3072, 384], P(('seq', 'ch'))
The draws below stay inside these ranges and needn't reach their ends.
All inputs are finite; a program needn't handle non-finite values.
Results may differ from the reference program's by a relative error of at most 0.025.
Values may be sent and summed in bfloat16 or wider, within the bound.
No kernel may reach another device: no remote copies, remote signals or barrier semaphores. Data moves between devices by JAX's collectives and lax.ppermute only.
A program may use at most 128 MiB of HBM per device.

```python
import math
import jax
import jax.numpy as jnp
from jax import lax

NB = 256
BS = 256
D = 1536
H = 3072
NBLK = 4
SEQL = 65536
DB = 384
HB = 768
N_CH = 8


def block_levels(rng, shape, cuts, smallest, largest):
    gain = 1.0
    for axis_at, shards_of in cuts:
        steps = jax.random.uniform(jax.random.fold_in(jax.random.fold_in(rng, 6), axis_at), (shards_of,), jnp.float32, smallest / len(cuts), largest / len(cuts))
        gain = gain * jnp.repeat(jnp.exp(steps), shape[axis_at] // shards_of).reshape((-1,) + (1,) * (len(shape) - 1 - axis_at))
    return gain


def scatter_about(rng, shape, scale, most, pieces=(), held_as=jnp.bfloat16):
    entries = jax.random.normal(rng, shape, jnp.float32) * scale
    if len(pieces) > 0:
        entries = block_levels(rng, shape, pieces, -0.22, 0.18) * entries
    return jnp.clip(entries, min=-most, max=most).astype(held_as)


def setup_inputs(seed: int = 0) -> dict:
    streams_of = jax.random.split(jax.random.key(seed), 10)
    return {
        "inputs": scatter_about(streams_of[0], (SEQL, D), 1.0, 6.0, ((0, 16), (1, 8))),
        "factor_one": scatter_about(streams_of[1], (NB, BS, BS), BS ** -0.5, 0.375, ((0, 16),)),
        "factor_two": scatter_about(streams_of[2], (BS, NB, NB), NB ** -0.5, 0.375, ((0, 16),)),
        "w_input_gate": scatter_about(streams_of[3], (D, DB), DB ** -0.5, 0.3125, ((0, 128),)),
        "norm_gain": jnp.clip(1.0 + 0.15 * jax.random.normal(streams_of[4], (D,), jnp.float32), 0.25, 1.75),
        "w_gate": scatter_about(streams_of[5], (D, HB), DB ** -0.5, 0.3125, ((0, 128),)),
        "w_up": scatter_about(streams_of[6], (D, HB), DB ** -0.5, 0.3125, ((0, 128),)),
        "w_down": scatter_about(streams_of[7], (H, DB), HB ** -0.5, 0.21875, ((0, 128),)),
        "grad_out": scatter_about(streams_of[8], (SEQL, D), 1.0, 6.0, ((0, 128),)),
    }


def silu_slope(value):
    sig = jax.nn.sigmoid(value)
    return sig * (1.0 + value * (1.0 - sig))

def held_round(value):
    rounded = lax.optimization_barrier(value.astype(jnp.bfloat16))
    return rounded.astype(jnp.float32)

def grouped_round(terms):
    rounded = terms.astype(jnp.bfloat16)
    rounded = lax.optimization_barrier(rounded)
    return lax.optimization_barrier(jnp.sum(rounded.astype(jnp.float32), axis=0))

def reference(inputs, factor_one, factor_two, w_input_gate, norm_gain, w_gate, w_up, w_down, grad_out):
    tok_scale = 1.0 / math.sqrt(SEQL)
    chan_scale = 1.0 / math.sqrt(D)
    input_f = inputs.astype(jnp.float32)
    blocks_in = input_f.reshape(NB, BS, D)
    fac_one = factor_one.astype(jnp.float32)
    fac_two = factor_two.astype(jnp.float32)
    first = jnp.einsum('iaj,ijc->iac', fac_one, blocks_in).astype(jnp.bfloat16)
    first_f = first.astype(jnp.float32)
    second = jnp.einsum('aki,iac->kac', fac_two, first_f).astype(jnp.bfloat16).reshape(SEQL, D)
    second_f = second.astype(jnp.float32)
    input3 = input_f.reshape(SEQL, NBLK, DB)
    win3 = w_input_gate.astype(jnp.float32).reshape(NBLK, DB, DB)
    pgate = jnp.einsum('tbd,bde->tbe', input3, win3).reshape(SEQL, D).astype(jnp.bfloat16)
    pgate_f = pgate.astype(jnp.float32)
    silu_in = jax.nn.silu(input_f)
    resid = (input_f + second_f * pgate_f * silu_in).astype(jnp.bfloat16)
    resid_f = resid.astype(jnp.float32)
    rstd = lax.rsqrt(lax.optimization_barrier(jnp.mean(resid_f * resid_f, axis=1, keepdims=True)) + 1e-06)
    normed = (resid_f * rstd * norm_gain).astype(jnp.bfloat16)
    normed3 = normed.astype(jnp.float32).reshape(SEQL, NBLK, DB)
    wg3 = w_gate.astype(jnp.float32).reshape(NBLK, DB, HB)
    wu3 = w_up.astype(jnp.float32).reshape(NBLK, DB, HB)
    wd3 = w_down.astype(jnp.float32).reshape(NBLK, HB, DB)
    gate = jnp.einsum('tbd,bdh->tbh', normed3, wg3)
    upper = jnp.einsum('tbd,bdh->tbh', normed3, wu3)
    sig = jax.nn.sigmoid(gate)
    hidden = (gate * sig * upper).astype(jnp.bfloat16)
    hidden_f = hidden.astype(jnp.float32)
    mixed_out = (resid_f + jnp.einsum('tbh,bhe->tbe', hidden_f, wd3).reshape(SEQL, D)).astype(jnp.bfloat16)
    cot = grad_out.astype(jnp.float32)
    cot3 = cot.reshape(SEQL, NBLK, DB)
    g_hidden = jnp.einsum('tbe,bhe->tbh', cot3, wd3)
    grad_w_down = jnp.einsum('tbh,tbe->bhe', hidden_f, cot3).reshape(H, DB) * tok_scale
    g_gate = (g_hidden * upper * sig * (1.0 + gate * (1.0 - sig))).astype(jnp.bfloat16).astype(jnp.float32)
    g_up = (g_hidden * gate * sig).astype(jnp.bfloat16).astype(jnp.float32)
    grad_w_gate = jnp.einsum('tbd,tbh->bdh', normed3, g_gate).reshape(D, HB) * tok_scale
    grad_w_up = jnp.einsum('tbd,tbh->bdh', normed3, g_up).reshape(D, HB) * tok_scale
    g_normed = (jnp.einsum('tbh,bdh->tbd', g_gate, wg3) + jnp.einsum('tbh,bdh->tbd', g_up, wu3)).reshape(SEQL, D)
    grad_norm_gain = lax.optimization_barrier(jnp.sum(g_normed * resid_f * rstd, axis=0)) * tok_scale
    scaled = g_normed * norm_gain
    g_resid = (cot + rstd * scaled - resid_f * rstd ** 3 * lax.optimization_barrier(jnp.mean(scaled * resid_f, axis=1, keepdims=True))).astype(jnp.bfloat16)
    resid_grad = g_resid.astype(jnp.float32)
    g_pgate = held_round(resid_grad * second_f * silu_in)
    g_pgate3 = g_pgate.reshape(SEQL, NBLK, DB)
    grad_w_input_gate = jnp.einsum('tbd,tbe->bde', input3, g_pgate3).reshape(D, DB) * tok_scale
    g_second = (resid_grad * pgate_f * silu_in).astype(jnp.bfloat16)
    through_gate = jnp.einsum('tbe,bde->tbd', g_pgate3, win3).reshape(SEQL, D)
    g_direct = held_round(resid_grad * (1.0 + second_f * pgate_f * silu_slope(input_f)) + through_gate)
    second_grad3 = g_second.astype(jnp.float32).reshape(NB, BS, D)
    g_first = jnp.einsum('aki,kac->iac', fac_two, second_grad3).astype(jnp.bfloat16)
    first_grad3 = g_first.astype(jnp.float32)
    groups = D // N_CH
    second_grad4 = second_grad3.reshape(NB, BS, N_CH, groups)
    first4 = first_f.reshape(NB, BS, N_CH, groups)
    two_terms = jnp.einsum('kagc,iagc->gaki', second_grad4, first4) * chan_scale
    grad_factor_two = grouped_round(two_terms)
    first_grad4 = first_grad3.reshape(NB, BS, N_CH, groups)
    blocks4 = blocks_in.reshape(NB, BS, N_CH, groups)
    one_terms = jnp.einsum('iagc,ijgc->giaj', first_grad4, blocks4) * chan_scale
    grad_factor_one = grouped_round(one_terms)
    back_in = jnp.einsum('iaj,iac->ijc', fac_one, first_grad3).reshape(SEQL, D)
    grad_inputs = (g_direct + back_in).astype(jnp.bfloat16)
    return (mixed_out, grad_inputs, grad_factor_one, grad_factor_two, grad_w_input_gate, grad_norm_gain, grad_w_gate, grad_w_up, grad_w_down)
```

```python
import math

import jax
import jax.numpy as jnp
from jax import lax
from jax.sharding import Mesh
from jax.sharding import PartitionSpec as P

D = 1536
NBLK = 4
SEQL = 65536
DB = D // NBLK
BF = jnp.bfloat16
F32 = jnp.float32

SEQ = ("zl", "y", "core")
CH = ("x", "zh")
ALL = SEQ + CH
SIZES = (2, 4, 2, 4, 2)
PLANE = SEQ + ("zh",)


def index_of(zl, y, k, x, zh):
    return (((zl * 4 + y) * 2 + k) * 4 + x) * 2 + zh


def shard_moves():
    moves = []
    for zl in range(2):
        for y in range(4):
            for k in range(2):
                for x in range(4):
                    for zh in range(2):
                        there = index_of(x // 2, (x % 2) * 2 + y % 2, k, zl * 2 + y // 2, zh)
                        moves.append((index_of(zl, y, k, x, zh), there))
    return moves


SWAP = [(0, 1), (1, 0)]


def silu_slope(value):
    sig = jax.nn.sigmoid(value)
    return sig * (1.0 + value * (1.0 - sig))


def sum_over_x(value):
    total = value
    for step in (1, 3, 2):
        total = total + lax.ppermute(value, "x", [(i, (i + step) % 4) for i in range(4)])
    return total


def exchange_x(parts):
    me = lax.axis_index("x")
    got = jnp.zeros_like(parts)
    own = lax.dynamic_index_in_dim(parts, me, 0, keepdims=True)
    got = lax.dynamic_update_slice_in_dim(got, own, me, 0)
    for step in (1, 3, 2):
        to = lax.rem(me + step, 4)
        frm = lax.rem(me + 4 - step, 4)
        piece = lax.dynamic_index_in_dim(parts, to, 0, keepdims=True)
        piece = lax.ppermute(piece, "x", [(i, (i + step) % 4) for i in range(4)])
        got = lax.dynamic_update_slice_in_dim(got, piece, frm, 0)
    return got


def per_device(
    inputs, factor_one, factor_two, w_input_gate, norm_gain, w_gate, w_up, w_down, grad_out
):
    tok_scale = 1.0 / math.sqrt(SEQL)
    chan_scale = 1.0 / math.sqrt(D)
    zh = lax.axis_index("zh")
    xi = lax.axis_index("x")

    payload = jnp.concatenate([w_gate, w_up, w_input_gate, w_down[:12], w_down[12:]], axis=1)
    payload = lax.ppermute(payload, ALL, shard_moves())
    gathered = lax.all_gather(payload, PLANE, axis=0, tiled=False)
    gathered = gathered.reshape(4, 2, 2, 2, 12, 2688).transpose(1, 2, 0, 3, 4, 5)
    upper_part = gathered[..., :1920].reshape(DB, 1920)
    wg, wu, win = upper_part[:, :768], upper_part[:, 768:1536], upper_part[:, 1536:]
    wd = gathered[..., 1920:].reshape(32, 12, 2, DB).transpose(0, 2, 1, 3).reshape(768, DB)
    gain = lax.dynamic_slice_in_dim(norm_gain, xi * DB, DB, 0)

    cot = exchange_x(grad_out.reshape(512, 4, DB).transpose(1, 0, 2)).reshape(2048, DB)
    halves = inputs.reshape(4, 2, 512, 192)
    mine = lax.dynamic_index_in_dim(halves, zh, 1, keepdims=False)
    other = lax.dynamic_index_in_dim(halves, 1 - zh, 1, keepdims=False)
    other = lax.ppermute(other, "zh", SWAP)
    input_mlp = jnp.where(
        zh == 0,
        jnp.concatenate([mine, other], axis=2),
        jnp.concatenate([other, mine], axis=2),
    ).reshape(2048, DB)

    def permuted(value):
        return value.reshape((4, 2, 2) + value.shape[1:]).swapaxes(0, 1).reshape(value.shape)

    f1 = permuted(factor_one)
    f1_half = lax.dynamic_slice_in_dim(f1, zh * 8, 8, 0)
    f2 = lax.dynamic_slice_in_dim(factor_two, zh * 8, 8, 0)
    f2 = f2.reshape(8, 16, 4, 2, 2, 16, 4, 2, 2).transpose(0, 1, 3, 2, 4, 5, 7, 6, 8)
    f2 = f2.reshape(8, 256, 256)

    token_blocks = permuted(inputs.reshape(16, 256, 192))
    first_local = jnp.einsum("iaj,ijc->iac", f1, token_blocks, preferred_element_type=F32)
    first_local = first_local.astype(BF).reshape(16, 32, 8, 192)
    piece = lax.all_to_all(first_local, PLANE, split_axis=1, concat_axis=0, tiled=False)
    first_cols = piece.reshape(16, 2, 16, 8, 192).transpose(0, 2, 3, 1, 4).reshape(256, 8, DB)
    second_cols = jnp.einsum("aki,iac->kac", f2, first_cols, preferred_element_type=F32)
    second_cols = second_cols.astype(BF).reshape(32, 8, 8, DB)
    second_mlp = lax.all_to_all(second_cols, PLANE, split_axis=0, concat_axis=1, tiled=False)
    second_mlp = second_mlp.reshape(2048, DB)

    pgate = jnp.dot(input_mlp, win, preferred_element_type=F32).astype(BF)
    pgate_f = pgate.astype(F32)
    input_f = input_mlp.astype(F32)
    silu_in = jax.nn.silu(input_f)
    second_f = second_mlp.astype(F32)
    resid = (input_f + second_f * pgate_f * silu_in).astype(BF)
    resid_f = resid.astype(F32)
    square = sum_over_x(jnp.sum(resid_f * resid_f, axis=1).reshape(16, 128)).reshape(2048, 1)
    rstd = lax.rsqrt(square * (1.0 / D) + 1e-06)
    normed = (resid_f * rstd * gain).astype(BF)
    gate = jnp.dot(normed, wg, preferred_element_type=F32)
    upper = jnp.dot(normed, wu, preferred_element_type=F32)
    sig = jax.nn.sigmoid(gate)
    hidden = (gate * sig * upper).astype(BF)
    down_out = jnp.dot(hidden, wd, preferred_element_type=F32)
    mixed = (resid_f + down_out).astype(BF)
    mixed_out = exchange_x(mixed.reshape(4, 512, DB)).transpose(1, 0, 2).reshape(512, D)
    g_hidden = jnp.einsum("te,he->th", cot, wd, preferred_element_type=F32)
    g_gate = (g_hidden * upper * sig * (1.0 + gate * (1.0 - sig))).astype(BF)
    g_up = (g_hidden * gate * sig).astype(BF)
    g_normed = jnp.einsum("th,dh->td", g_gate, wg, preferred_element_type=F32)
    g_normed = g_normed + jnp.einsum("th,dh->td", g_up, wu, preferred_element_type=F32)
    gain_term = jnp.sum(g_normed * resid_f * rstd, axis=0)
    scaled = g_normed * gain
    inner = sum_over_x(jnp.sum(scaled * resid_f, axis=1).reshape(16, 128)).reshape(2048, 1)
    cot_f = cot.astype(F32)
    g_resid = (cot_f + rstd * scaled - resid_f * rstd**3 * (inner * (1.0 / D))).astype(BF)
    resid_grad = g_resid.astype(F32)
    g_pgate = (resid_grad * second_f * silu_in).astype(BF)
    g_second = (resid_grad * pgate_f * silu_in).astype(BF)
    through_gate = jnp.einsum("te,de->td", g_pgate, win, preferred_element_type=F32)
    g_direct = (
        resid_grad * (1.0 + second_f * pgate_f * silu_slope(input_f)) + through_gate
    ).astype(BF)

    term_gate = jnp.einsum("td,th->dh", normed, g_gate, preferred_element_type=F32)
    term_up = jnp.einsum("td,th->dh", normed, g_up, preferred_element_type=F32)
    term_down = jnp.einsum("th,te->he", hidden, cot, preferred_element_type=F32)
    term_entry = jnp.einsum("td,te->de", input_mlp, g_pgate, preferred_element_type=F32)
    down2 = term_down.reshape(32, 2, 12, DB).transpose(0, 2, 1, 3).reshape(DB, 2 * DB)
    terms = jnp.concatenate([term_gate, term_up, term_entry, down2], axis=1).astype(BF)
    terms = terms.reshape(2, 2, 4, 2, 12, 2688).transpose(2, 0, 1, 3, 4, 5).reshape(32, 12, 2688)
    gain_row = jnp.pad(gain_term.astype(BF), (0, 2688 - DB)).reshape(1, 1, 2688)
    terms = jnp.concatenate([terms, jnp.broadcast_to(gain_row, (32, 1, 2688))], axis=1)
    by_core = terms.reshape(8, 2, 2, 13, 2688).swapaxes(0, 1).reshape(2, 16, 13, 2688)
    me = lax.axis_index("core")
    keep = lax.dynamic_index_in_dim(by_core, me, 0, keepdims=False)
    give = lax.dynamic_index_in_dim(by_core, 1 - me, 0, keepdims=False)
    pair = (keep.astype(F32) + lax.ppermute(give, "core", SWAP).astype(F32)).astype(BF)
    pair = lax.all_to_all(pair, ("zl", "y", "zh"), split_axis=0, concat_axis=0, tiled=True)
    summed = jnp.sum(pair.astype(F32), axis=0) * tok_scale
    back = [(there, here) for here, there in shard_moves()]
    own = lax.ppermute(summed[:12], ALL, back)
    grad_w_gate, grad_w_up = own[:, :768], own[:, 768:1536]
    grad_w_input_gate = own[:, 1536:1920]
    grad_w_down = jnp.concatenate([own[:, 1920:2304], own[:, 2304:]], axis=0)
    gain_here = summed[12, :DB].reshape(1, DB)
    grad_norm_gain = exchange_x(jnp.broadcast_to(gain_here, (4, DB))).reshape(D)

    piece = g_second.reshape(8, 32, 8, DB)
    piece = lax.all_to_all(piece, PLANE, split_axis=1, concat_axis=0, tiled=False)
    second_grad = piece.reshape(256, 8, DB)
    first_grad = jnp.einsum("aki,kac->iac", f2, second_grad, preferred_element_type=F32)
    first_grad = first_grad.astype(BF).reshape(32, 8, 8, DB)
    term_two = jnp.einsum("kac,iac->aki", second_grad, first_cols, preferred_element_type=F32)
    term_two = (term_two * chan_scale).astype(BF)
    term_two = term_two.reshape(8, 16, 2, 4, 2, 16, 2, 4, 2).transpose(0, 1, 3, 2, 4, 5, 7, 6, 8)
    term_two = term_two.reshape(8, 8, 32, 256)
    term_two = lax.all_to_all(term_two, CH, split_axis=1, concat_axis=0, tiled=False)
    grad_factor_two = jnp.sum(term_two.reshape(4, 16, 32, 256).astype(F32), axis=0)

    g_first = lax.all_to_all(first_grad, PLANE, split_axis=0, concat_axis=1, tiled=False)
    g_first = g_first.reshape(8, 256, DB)
    in_blocks = input_mlp.reshape(8, 256, DB)
    term_one = jnp.einsum("iac,ijc->iaj", g_first, in_blocks, preferred_element_type=F32)
    term_one = (term_one * chan_scale).astype(BF).reshape(8, 8, 32, 256)
    term_one = lax.all_to_all(term_one, CH, split_axis=1, concat_axis=0, tiled=False)
    grad_factor_one = jnp.sum(term_one.reshape(4, 2, 8, 32, 256).astype(F32), axis=0)
    grad_factor_one = grad_factor_one.reshape(2, 4, 2, 32, 256).swapaxes(0, 1).reshape(16, 32, 256)

    back_in = jnp.einsum("iaj,iac->ijc", f1_half, g_first, preferred_element_type=F32)
    total = (g_direct.astype(F32) + back_in.reshape(2048, DB)).astype(BF)
    total = total.reshape(4, 512, 2, 192)
    mine = lax.dynamic_index_in_dim(total, zh, 2, keepdims=False)
    other = lax.dynamic_index_in_dim(total, 1 - zh, 2, keepdims=False)
    other = lax.ppermute(other, "zh", SWAP)
    grad_inputs = jnp.where(
        zh == 0, jnp.stack([mine, other], axis=1), jnp.stack([other, mine], axis=1)
    ).reshape(4096, 192)
    return (
        mixed_out,
        grad_inputs,
        grad_factor_one,
        grad_factor_two,
        grad_w_input_gate,
        grad_norm_gain,
        grad_w_gate,
        grad_w_up,
        grad_w_down,
    )


def solution(mesh):
    fine = Mesh(mesh.devices.reshape(SIZES), ALL)
    return jax.shard_map(
        per_device,
        mesh=fine,
        in_specs=(
            P(SEQ, CH),
            P(SEQ, None, None),
            P(SEQ, None, None),
            P(ALL, None),
            P(),
            P(ALL, None),
            P(ALL, None),
            P(ALL, None),
            P(ALL, None),
        ),
        out_specs=(
            P(ALL, None),
            P(SEQ, CH),
            P(SEQ, CH, None),
            P(SEQ, CH, None),
            P(ALL, None),
            P(),
            P(ALL, None),
            P(ALL, None),
            P(ALL, None),
        ),
        check_vma=False,
    )
```

```python
import math

import jax
import jax.numpy as jnp
from jax import lax
from jax.experimental import pallas as pl
from jax.experimental.pallas import tpu as pltpu
from jax.sharding import Mesh
from jax.sharding import PartitionSpec as P

D = 1536
NBLK = 4
SEQL = 65536
DB = D // NBLK
BF = jnp.bfloat16
F32 = jnp.float32

SEQ = ("zl", "y", "core")
CH = ("x", "zh")
ALL = SEQ + CH
SIZES = (2, 4, 2, 4, 2)
PLANE = SEQ + ("zh",)


def index_of(zl, y, k, x, zh):
    return (((zl * 4 + y) * 2 + k) * 4 + x) * 2 + zh


def shard_moves():
    moves = []
    for zl in range(2):
        for y in range(4):
            for k in range(2):
                for x in range(4):
                    for zh in range(2):
                        there = index_of(k, x, y % 2, zl * 2 + y // 2, zh)
                        moves.append((index_of(zl, y, k, x, zh), there))
    return moves


SWAP = [(0, 1), (1, 0)]


def call(body, grid, ins, outs, shapes, cost, scratch=()):
    return pl.pallas_call(
        body,
        grid_spec=pltpu.PrefetchScalarGridSpec(
            num_scalar_prefetch=1,
            grid=grid,
            in_specs=ins,
            out_specs=outs,
            scratch_shapes=list(scratch),
        ),
        out_shape=shapes,
        compiler_params=pltpu.CompilerParams(
            dimension_semantics=("arbitrary",) * len(grid), vmem_limit_bytes=56 * 1024 * 1024
        ),
        cost_estimate=pl.CostEstimate(flops=cost[0], bytes_accessed=cost[1], transcendentals=0),
    )


def whole(*shape):
    return pl.BlockSpec(shape, lambda t, s: (0,) * len(shape))


def rows(width, height=512):
    return pl.BlockSpec((height, width), lambda t, s: (t, 0))


def lead(*shape):
    return pl.BlockSpec((1,) + shape, lambda t, s: (t,) + (0,) * len(shape))


PIECES = pl.BlockSpec((32, 2, 8, DB), lambda t, s: (0, t, 0, 0))


def read_pieces(ref):
    return jnp.concatenate(
        [ref[:, r].astype(F32).reshape(256, DB) for r in range(2)], axis=0
    )


def row_sums(value):
    ones = jnp.ones((8, DB), BF)
    total = jnp.zeros((8, value.shape[0]), F32)
    for _ in range(3):
        part = value.astype(BF)
        total = total + lax.dot_general(
            ones, part, (((1,), (1,)), ((), ())), preferred_element_type=F32
        )
        value = value - part.astype(F32)
    return total


def as_column(row):
    turned = jnp.transpose(jnp.broadcast_to(row, (128, row.shape[1])))
    return jnp.concatenate([turned] * (DB // 128), axis=1)


def dot(a, b):
    return jnp.dot(a, b, preferred_element_type=F32)


def dot_t(a, b):
    return lax.dot_general(a, b, (((1,), (1,)), ((), ())), preferred_element_type=F32)


def first_kernel(_, f1_ref, in_ref, out_ref):
    results = [
        dot(f1_ref[r], in_ref[r * 256 : (r + 1) * 256]).reshape(32, 8, 192) for r in range(2)
    ]
    out_ref[:, 0] = jnp.concatenate(results, axis=2).astype(BF)


def give_kernel(_, in_ref, out_ref):
    value = in_ref[0]
    out_ref[...] = jnp.concatenate([value[:256], value[256:]], axis=1)


def put_rows(refs, row, value):
    for j, ref in enumerate(refs):
        ref[row : row + value.shape[0], :] = value[:, j * 128 : (j + 1) * 128]


def put_position(refs, a, value):
    for j, ref in enumerate(refs):
        ref[pl.ds(a, 256, stride=8), :] = value[:, j * 128 : (j + 1) * 128]


def take_position(refs, a):
    parts = [ref[pl.ds(a, 256, stride=8), :] for ref in refs]
    return jnp.concatenate(parts, axis=1).astype(BF)


def second_kernel(_, piece_ref, f2_ref, out_ref, first_ref, *scratch):
    cols, result = scratch[:3], scratch[3:]
    for s in range(16):
        for pair in range(8):
            low, high = (piece_ref[2 * s + h, pair].astype(F32) for h in range(2))
            row = (s * 16 + pair * 2) * 8
            put_rows(cols, row, jnp.concatenate([low[:, :192], high[:, :192]], axis=1))
            put_rows(cols, row + 8, jnp.concatenate([low[:, 192:], high[:, 192:]], axis=1))
    for a in range(8):
        first = take_position(cols, a)
        first_ref[a] = first
        put_position(result, a, dot(f2_ref[a], first))
    write_blocks(result, out_ref)


def first_grad_kernel(_, piece_ref, f2_ref, out_ref, grad_ref, *scratch):
    cols, result = scratch[:3], scratch[3:]
    for dev in range(32):
        s, h = dev // 2, dev % 2
        for x in range(4):
            row = (s * 16 + x * 4 + h * 2) * 8
            put_rows(cols, row, piece_ref[dev, 2 * x : 2 * x + 2].astype(F32).reshape(16, DB))
    for a in range(8):
        grad = take_position(cols, a)
        grad_ref[a] = grad
        put_position(result, a, lax.dot_general(
            f2_ref[a], grad, (((0,), (0,)), ((), ())), preferred_element_type=F32
        ))
    write_blocks(result, out_ref)


def write_blocks(result, out_ref):
    for dev in range(32):
        s, h = dev // 2, dev % 2
        for x in range(4):
            row = (s * 16 + x * 4 + h * 2) * 8
            value = jnp.concatenate([ref[row : row + 16, :] for ref in result], axis=1)
            out_ref[dev, 2 * x : 2 * x + 2] = value.reshape(2, 8, DB).astype(BF)


def gating_kernel(zh_ref, own_ref, got_ref, second_ref, win_ref, in_ref, resid_ref, pgate_ref, sum_ref):
    zh = zh_ref[0]
    own = own_ref[0]
    got = jnp.concatenate([got_ref[:, :192], got_ref[:, 192:]], axis=0)
    first_half = jnp.where(zh == 0, own, got)
    second_half = jnp.where(zh == 0, got, own)
    value = jnp.concatenate([first_half, second_half], axis=1)
    in_ref[...] = value
    pgate = dot(value, win_ref[...]).astype(BF)
    pgate_ref[...] = pgate
    value_f = value.astype(F32)
    silu_in = value_f * jax.nn.sigmoid(value_f)
    resid = (value_f + read_pieces(second_ref) * pgate.astype(F32) * silu_in).astype(BF)
    resid_ref[...] = resid
    resid_f = resid.astype(F32)
    sum_ref[0] = row_sums(resid_f * resid_f)


def mlp_kernel(
    _, resid_ref, cot_ref, square_ref, gain_ref, wg_ref, wu_ref, wd_ref,
    mixed_ref, normed_ref, hidden_ref, grads_ref, gnormed_ref, inner_ref, gain_out_ref,
):
    resid_f = resid_ref[...].astype(F32)
    rstd = as_column(lax.rsqrt(square_ref[0] * (1.0 / D) + 1e-06))
    gain = gain_ref[...]
    scaled_resid = resid_f * rstd
    normed = (scaled_resid * gain).astype(BF)
    normed_ref[...] = normed
    gate = dot(normed, wg_ref[...])
    upper = dot(normed, wu_ref[...])
    g_hidden = dot_t(cot_ref[0], wd_ref[...])
    sig = jax.nn.sigmoid(gate)
    act = gate * sig
    hidden = (act * upper).astype(BF)
    hidden_ref[...] = hidden
    g_gate = (g_hidden * upper * sig * (1.0 + gate * (1.0 - sig))).astype(BF)
    g_up = (g_hidden * act).astype(BF)
    grads_ref[:, :768] = g_gate
    grads_ref[:, 768:] = g_up
    mixed_ref[0] = (resid_f + dot(hidden, wd_ref[...])).astype(BF)
    g_normed = dot_t(g_gate, wg_ref[...]) + dot_t(g_up, wu_ref[...])
    gnormed_ref[...] = g_normed
    inner_ref[0] = row_sums(g_normed * gain * resid_f)
    term = jnp.sum((g_normed * scaled_resid).reshape(64, 8, DB), axis=0)

    @pl.when(pl.program_id(0) == 0)
    def _():
        gain_out_ref[...] = jnp.zeros_like(gain_out_ref)

    gain_out_ref[...] += term


def resid_grad_kernel(
    _, resid_ref, cot_ref, square_ref, inner_ref, gain_ref, gnormed_ref, in_ref, pgate_ref,
    g_resid_ref, g_second_ref,
):
    rstd_row = lax.rsqrt(square_ref[0] * (1.0 / D) + 1e-06)
    rstd = as_column(rstd_row)
    factor = as_column(rstd_row * rstd_row * rstd_row * (inner_ref[0] * (1.0 / D)))
    scaled = gnormed_ref[...] * gain_ref[...]
    g_resid = (
        cot_ref[0].astype(F32) + rstd * scaled - resid_ref[...].astype(F32) * factor
    ).astype(BF)
    g_resid_ref[...] = g_resid
    value = in_ref[...].astype(F32)
    silu_in = value * jax.nn.sigmoid(value)
    g_second = (g_resid.astype(F32) * pgate_ref[...].astype(F32) * silu_in).astype(BF)
    for r in range(2):
        g_second_ref[:, r] = g_second[r * 256 : (r + 1) * 256].reshape(32, 8, DB)


def direct_kernel(_, g_resid_ref, in_ref, second_ref, pgate_ref, win_ref, g_direct_ref, term_ref):
    resid_grad = g_resid_ref[...].astype(F32)
    value = in_ref[...].astype(F32)
    sig = jax.nn.sigmoid(value)
    second = read_pieces(second_ref)
    g_pgate = (resid_grad * second * (value * sig)).astype(BF)
    slope = sig * (1.0 + value * (1.0 - sig))
    through = dot_t(g_pgate, win_ref[...])
    g_direct_ref[...] = (
        resid_grad * (1.0 + second * pgate_ref[...].astype(F32) * slope) + through
    ).astype(BF)
    term = lax.dot_general(
        in_ref[...], g_pgate, (((0,), (0,)), ((), ())), preferred_element_type=F32
    )

    @pl.when(pl.program_id(0) == 0)
    def _():
        term_ref[...] = jnp.zeros_like(term_ref)

    term_ref[...] += term


def back_kernel(zh_ref, g_first_ref, in_ref, f1_ref, direct_ref, term_ref, own_ref, give_ref):
    zh = zh_ref[0]
    gives = []
    for r in range(2):
        here = slice(r * 256, (r + 1) * 256)
        g_first = g_first_ref[:, r].reshape(256, DB)
        term = dot_t(g_first, in_ref[here]) * (1.0 / math.sqrt(D))
        term_ref[:, r] = term.astype(BF).reshape(8, 32, 256)
        back = lax.dot_general(
            f1_ref[0, r], g_first, (((0,), (0,)), ((), ())), preferred_element_type=F32
        )
        total = direct_ref[here].astype(F32) + back
        low, high = total[:, :192], total[:, 192:]
        own_ref[here] = jnp.where(zh == 0, low, high).astype(BF)
        gives.append(jnp.where(zh == 0, high, low))
    give_ref[...] = jnp.concatenate(gives, axis=1).astype(BF)


def join_kernel(zh_ref, own_ref, got_ref, out_ref):
    zh = zh_ref[0]
    own = own_ref[...]
    got = jnp.concatenate([got_ref[:, :192], got_ref[:, 192:]], axis=0)
    out_ref[:512] = jnp.where(zh == 0, own, got)
    out_ref[512:] = jnp.where(zh == 0, got, own)


def factor_sum_kernel(_, term_ref, out_ref):
    for h in range(2):
        total = term_ref[h].astype(F32)
        for x in range(1, 4):
            total = total + term_ref[2 * x + h].astype(F32)
        out_ref[0, h] = total


def factor_sum_two_kernel(_, term_ref, out_ref):
    for h in range(2):
        total = term_ref[h].astype(F32)
        for x in range(1, 4):
            total = total + term_ref[2 * x + h].astype(F32)
        out_ref[h] = total


def around_x(value):
    steps = [lax.ppermute(value, "x", [(i, (i + step) % 4) for i in range(4)]) for step in (1, 3, 2)]
    return [value, steps[0], steps[2], steps[1]]


def per_device(
    inputs, factor_one, factor_two, w_input_gate, norm_gain, w_gate, w_up, w_down, grad_out
):
    tok_scale = 1.0 / math.sqrt(SEQL)
    chan_scale = 1.0 / math.sqrt(D)
    zh = lax.axis_index("zh")
    xi = lax.axis_index("x")
    core = lax.axis_index("core")
    zh_arg = zh.reshape(1).astype(jnp.int32)
    bf = lambda *shape: jax.ShapeDtypeStruct(shape, BF)
    f32 = lambda *shape: jax.ShapeDtypeStruct(shape, F32)

    first_local = call(
        first_kernel, (8,),
        [pl.BlockSpec((2, 256, 256), lambda t, s: (t, 0, 0)), rows(192)],
        pl.BlockSpec((32, 1, 8, DB), lambda t, s: (0, t, 0, 0)),
        bf(32, 8, 8, DB),
        (400_000_000, 6_000_000),
    )(zh_arg, factor_one, inputs)
    piece = lax.all_to_all(first_local, PLANE, split_axis=0, concat_axis=0, tiled=True)

    payload = jnp.concatenate([w_gate, w_up, w_input_gate, w_down[:12], w_down[12:]], axis=1)
    payload = lax.ppermute(payload, ALL, shard_moves())
    payload = jnp.broadcast_to(payload, (16, 12, 2688))
    payload = lax.all_to_all(payload, ("zl", "y", "zh"), split_axis=0, concat_axis=0, tiled=True)
    across = lax.ppermute(payload, "core", SWAP)
    gathered = jnp.concatenate(
        [jnp.where(core == 0, payload, across), jnp.where(core == 0, across, payload)], axis=0
    )
    upper_part = gathered[..., :1920].reshape(DB, 1920)
    wg, wu, win = upper_part[:, :768], upper_part[:, 768:1536], upper_part[:, 1536:]
    wd = gathered[..., 1920:].reshape(32, 12, 2, DB).transpose(0, 2, 1, 3).reshape(768, DB)
    gain = lax.dynamic_slice_in_dim(norm_gain, xi * DB, DB, 0).reshape(1, DB)

    cot = lax.all_to_all(
        grad_out.reshape(512, 4, DB).transpose(1, 0, 2), "x", split_axis=0, concat_axis=0, tiled=True
    )
    packed = rows(DB, 256)
    give = call(
        give_kernel, (4,),
        [pl.BlockSpec((1, 512, 192), lambda t, s: (2 * t + 1 - s[0], 0, 0))],
        packed, bf(1024, DB), (1, 2_000_000),
    )(zh_arg, inputs.reshape(8, 512, 192))
    other = lax.ppermute(give, "zh", SWAP)
    f2 = lax.dynamic_slice_in_dim(factor_two, zh * 8, 8, 0)

    wide = [pltpu.VMEM((2048, 128), F32)] * 6
    all_pieces = whole(32, 8, 8, DB)
    second_cols, first_cols = call(
        second_kernel, (1,),
        [all_pieces, whole(8, 256, 256)],
        [all_pieces, whole(8, 256, DB)],
        [bf(32, 8, 8, DB), bf(8, 256, DB)],
        (400_000_000, 6_000_000), wide,
    )(zh_arg, piece, f2)
    second = lax.all_to_all(second_cols, PLANE, split_axis=0, concat_axis=0, tiled=True)

    chunk = pl.BlockSpec((1, 512, 192), lambda t, s: (2 * t + s[0], 0, 0))
    input_mlp, resid, pgate, square = call(
        gating_kernel, (4,),
        [chunk, packed, PIECES, whole(DB, DB)],
        [rows(DB), rows(DB), rows(DB), lead(8, 512)],
        [bf(2048, DB), bf(2048, DB), bf(2048, DB), f32(4, 8, 512)],
        (600_000_000, 10_000_000),
    )(zh_arg, inputs.reshape(8, 512, 192), other, second, win)
    square = sum(around_x(square[:, 0])).reshape(4, 1, 512)
    mixed, normed, hidden, grads, g_normed, inner, gain_term = call(
        mlp_kernel, (4,),
        [rows(DB), lead(512, DB), lead(1, 512), whole(1, DB), whole(DB, 768), whole(DB, 768), whole(768, DB)],
        [lead(512, DB), rows(DB), rows(768), rows(1536), rows(DB), lead(8, 512), whole(8, DB)],
        [bf(4, 512, DB), bf(2048, DB), bf(2048, 768), bf(2048, 1536), f32(2048, DB), f32(4, 8, 512), f32(8, DB)],
        (7_300_000_000, 24_000_000),
    )(zh_arg, resid, cot, square, gain, wg, wu, wd)
    gain_here = jnp.pad(jnp.sum(gain_term, axis=0), (0, 128)).reshape(1, 512)
    sums = around_x(jnp.concatenate([inner[:, 0], gain_here], axis=0))
    inner = sum(v[:4] for v in sums).reshape(4, 1, 512)
    gain_terms = jnp.concatenate([v[4:, :DB] for v in sums[::-1]] * 2, axis=0)
    gain_terms = lax.dynamic_slice_in_dim(gain_terms, lax.rem(7 - xi, 4), 4, 0).reshape(D)
    g_resid, g_second = call(
        resid_grad_kernel, (4,),
        [rows(DB), lead(512, DB), lead(1, 512), lead(1, 512), whole(1, DB), rows(DB), rows(DB), rows(DB)],
        [rows(DB), PIECES],
        [bf(2048, DB), bf(32, 8, 8, DB)],
        (50_000_000, 12_000_000),
    )(zh_arg, resid, cot, square, inner, gain, g_normed, input_mlp, pgate)
    piece = lax.all_to_all(g_second, PLANE, split_axis=0, concat_axis=0, tiled=True)
    mixed, g_resid = lax.optimization_barrier((mixed, g_resid))
    mixed_out = lax.all_to_all(mixed, "x", split_axis=0, concat_axis=0, tiled=True)
    mixed_out = mixed_out.transpose(1, 0, 2).reshape(512, D)
    g_direct, term_entry = call(
        direct_kernel, (4,),
        [rows(DB), rows(DB), PIECES, rows(DB), whole(DB, DB)],
        [rows(DB), whole(DB, DB)],
        [bf(2048, DB), f32(DB, DB)],
        (1_200_000_000, 10_000_000),
    )(zh_arg, g_resid, input_mlp, second, pgate, win)

    term_gu = jnp.einsum("td,th->dh", normed, grads, preferred_element_type=F32)
    term_down = jnp.einsum("th,te->he", hidden, cot.reshape(2048, DB), preferred_element_type=F32)
    down2 = term_down.astype(BF).reshape(32, 2, 12, DB).transpose(0, 2, 1, 3).reshape(32, 12, 2 * DB)
    terms = jnp.concatenate([term_gu, term_entry], axis=1).astype(BF).reshape(32, 12, 1920)
    terms = jnp.concatenate([terms, down2], axis=2)
    gain_row = jnp.pad(gain_terms.astype(BF), (0, 2688 - D)).reshape(1, 1, 2688)
    terms = jnp.concatenate([terms, jnp.broadcast_to(gain_row, (32, 1, 2688))], axis=1)
    keep = lax.dynamic_slice_in_dim(terms, core * 16, 16, 0)
    give = lax.dynamic_slice_in_dim(terms, (1 - core) * 16, 16, 0)
    pair = (keep.astype(F32) + lax.ppermute(give, "core", SWAP).astype(F32)).astype(BF)
    pair, piece = lax.optimization_barrier((pair, piece))
    pair = lax.all_to_all(pair, ("zl", "y", "zh"), split_axis=0, concat_axis=0, tiled=True)
    summed = jnp.sum(pair.astype(F32), axis=0) * tok_scale
    back = [(there, here) for here, there in shard_moves()]
    own = lax.ppermute(summed[:12], ALL, back)
    grad_w_gate, grad_w_up = own[:, :768], own[:, 768:1536]
    grad_w_input_gate = own[:, 1536:1920]
    grad_w_down = jnp.concatenate([own[:, 1920:2304], own[:, 2304:]], axis=0)
    grad_norm_gain = summed[12, :D]

    first_grad, second_grad = call(
        first_grad_kernel, (1,),
        [all_pieces, whole(8, 256, 256)],
        [all_pieces, whole(8, 256, DB)],
        [bf(32, 8, 8, DB), bf(8, 256, DB)],
        (400_000_000, 6_000_000), wide,
    )(zh_arg, piece, f2)
    g_first = lax.all_to_all(first_grad, PLANE, split_axis=0, concat_axis=0, tiled=True)
    term_two = jnp.einsum("akc,aic->aki", second_grad, first_cols, preferred_element_type=F32)
    term_two = (term_two * chan_scale).astype(BF).reshape(8, 8, 32, 256)
    term_two = lax.all_to_all(term_two.swapaxes(0, 1), CH, split_axis=0, concat_axis=0, tiled=True)
    term_in = pl.BlockSpec((8, 2, 32, 256), lambda t, s: (0, t, 0, 0))
    grad_factor_two = call(
        factor_sum_two_kernel, (4,), [term_in],
        pl.BlockSpec((2, 2, 32, 256), lambda t, s: (0, t, 0, 0)),
        f32(2, 8, 32, 256), (1, 3_000_000),
    )(zh_arg, term_two).reshape(16, 32, 256)

    term_one, own_grad, give_grad = call(
        back_kernel, (4,),
        [PIECES, rows(DB), pl.BlockSpec((1, 2, 256, 256), lambda t, s: (2 * t + s[0], 0, 0, 0)), rows(DB)],
        [term_in, rows(192), packed],
        [bf(8, 8, 32, 256), bf(2048, 192), bf(1024, DB)],
        (800_000_000, 9_000_000),
    )(zh_arg, g_first, input_mlp, factor_one.reshape(8, 2, 256, 256), g_direct)
    got_grad = lax.ppermute(give_grad, "zh", SWAP)
    term_one = lax.all_to_all(term_one, CH, split_axis=0, concat_axis=0, tiled=True)
    grad_factor_one = call(
        factor_sum_kernel, (4,), [term_in],
        pl.BlockSpec((1, 2, 2, 32, 256), lambda t, s: (t, 0, 0, 0, 0)),
        f32(4, 2, 2, 32, 256), (1, 3_000_000),
    )(zh_arg, term_one).reshape(16, 32, 256)
    grad_inputs = call(
        join_kernel, (4,), [rows(192), packed], rows(192, 1024), bf(4096, 192), (1, 4_000_000)
    )(zh_arg, own_grad, got_grad)
    return (
        mixed_out,
        grad_inputs,
        grad_factor_one,
        grad_factor_two,
        grad_w_input_gate,
        grad_norm_gain,
        grad_w_gate,
        grad_w_up,
        grad_w_down,
    )


def solution(mesh):
    fine = Mesh(mesh.devices.reshape(SIZES), ALL)
    return jax.shard_map(
        per_device,
        mesh=fine,
        in_specs=(
            P(SEQ, CH),
            P(SEQ, None, None),
            P(SEQ, None, None),
            P(ALL, None),
            P(),
            P(ALL, None),
            P(ALL, None),
            P(ALL, None),
            P(ALL, None),
        ),
        out_specs=(
            P(ALL, None),
            P(SEQ, CH),
            P(SEQ, CH, None),
            P(SEQ, CH, None),
            P(ALL, None),
            P(),
            P(ALL, None),
            P(ALL, None),
            P(ALL, None),
        ),
        check_vma=False,
    )
```

```python
import math

import jax
import jax.numpy as jnp
from jax import lax
from jax.experimental import pallas as pl
from jax.experimental.pallas import tpu as pltpu
from jax.sharding import Mesh
from jax.sharding import PartitionSpec as P

D = 1536
NBLK = 4
SEQL = 65536
DB = D // NBLK
BF = jnp.bfloat16
F32 = jnp.float32

SEQ = ("zl", "y", "core")
CH = ("x", "zh")
ALL = SEQ + CH
SIZES = (2, 4, 2, 4, 2)
PLANE = SEQ + ("zh",)


def index_of(zl, y, k, x, zh):
    return (((zl * 4 + y) * 2 + k) * 4 + x) * 2 + zh


def shard_moves():
    moves = []
    for zl in range(2):
        for y in range(4):
            for k in range(2):
                for x in range(4):
                    for zh in range(2):
                        there = index_of(k, x, y % 2, zl * 2 + y // 2, zh)
                        moves.append((index_of(zl, y, k, x, zh), there))
    return moves


SWAP = [(0, 1), (1, 0)]


def call(body, grid, ins, outs, shapes, cost, scratch=()):
    return pl.pallas_call(
        body,
        grid_spec=pltpu.PrefetchScalarGridSpec(
            num_scalar_prefetch=1,
            grid=grid,
            in_specs=ins,
            out_specs=outs,
            scratch_shapes=list(scratch),
        ),
        out_shape=shapes,
        name=body.__name__,
        compiler_params=pltpu.CompilerParams(
            dimension_semantics=("arbitrary",) * len(grid), vmem_limit_bytes=56 * 1024 * 1024
        ),
        cost_estimate=pl.CostEstimate(flops=cost[0], bytes_accessed=cost[1], transcendentals=0),
    )


def whole(*shape):
    return pl.BlockSpec(shape, lambda t, s: (0,) * len(shape))


def rows(width, height=512):
    return pl.BlockSpec((height, width), lambda t, s: (t, 0))


def turned_rows(width, height=512):
    return pl.BlockSpec((height, width), lambda t, s: (lax.rem(s[1] + t, 4), 0))


def columns(height, width=512):
    return pl.BlockSpec((height, width), lambda t, s: (0, t))


PIECES = pl.BlockSpec((32, 2, 8, DB), lambda t, s: (0, t, 0, 0))
SUMS = [whole(8, 512)] * 4


def read_pieces(ref):
    return jnp.concatenate(
        [ref[:, r].astype(F32).reshape(256, DB) for r in range(2)], axis=0
    )


def row_sums(value):
    ones = jnp.ones((8, DB), BF)
    high = value.astype(BF)
    low = (value - high.astype(F32)).astype(BF)
    return dot_t(ones, high) + dot_t(ones, low)


def row_of(refs, at):
    total = refs[0][...] + refs[1][...] + refs[2][...] + refs[3][...]
    here = lax.broadcasted_iota(jnp.int32, (8, 512), 0) == at
    return jnp.sum(jnp.where(here, total, 0.0), axis=0, keepdims=True)


def put_row(ref, at, value):
    here = lax.broadcasted_iota(jnp.int32, (8, 512), 0) == at
    ref[...] = jnp.where(here, value, ref[...])


def as_column(row):
    turned = jnp.transpose(jnp.broadcast_to(row, (128, row.shape[1])))
    return jnp.concatenate([turned] * (DB // 128), axis=1)


def dot(a, b):
    return jnp.dot(a, b, preferred_element_type=F32)


def dot_t(a, b):
    return lax.dot_general(a, b, (((1,), (1,)), ((), ())), preferred_element_type=F32)


def t_dot(a, b):
    return lax.dot_general(a, b, (((0,), (0,)), ((), ())), preferred_element_type=F32)


def first_kernel(_, f1_ref, in_ref, out_ref):
    results = [
        dot_t(f1_ref[r], in_ref[:, r * 256 : (r + 1) * 256]).reshape(32, 8, 192) for r in range(2)
    ]
    out_ref[:, 0] = jnp.concatenate(results, axis=2).astype(BF)


def copy_kernel(_, in_ref, out_ref):
    out_ref[...] = in_ref[...]


def copy_three_kernel(_, *refs):
    for j in range(3):
        refs[3 + j][...] = refs[j][...]


def put_rows(refs, row, value):
    for j, ref in enumerate(refs):
        ref[row : row + value.shape[0], :] = value[:, j * 128 : (j + 1) * 128]


def put_position(refs, a, value):
    for j, ref in enumerate(refs):
        ref[pl.ds(a, 256, stride=8), :] = value[:, j * 128 : (j + 1) * 128]


def take_position(refs, a):
    parts = [ref[pl.ds(a, 256, stride=8), :] for ref in refs]
    return jnp.concatenate(parts, axis=1).astype(BF)


def second_kernel(_, piece_ref, f2_ref, out_ref, first_ref, *scratch):
    cols, result = scratch[:3], scratch[3:]
    for s in range(16):
        for pair in range(8):
            low, high = (piece_ref[2 * s + h, pair].astype(F32) for h in range(2))
            row = (s * 16 + pair * 2) * 8
            put_rows(cols, row, jnp.concatenate([low[:, :192], high[:, :192]], axis=1))
            put_rows(cols, row + 8, jnp.concatenate([low[:, 192:], high[:, 192:]], axis=1))
    for a in range(8):
        first = take_position(cols, a)
        first_ref[a] = first
        put_position(result, a, dot(f2_ref[a], first))
    write_blocks(result, out_ref)


def first_grad_kernel(_, piece_ref, f2_ref, out_ref, grad_ref, *scratch):
    cols, result = scratch[:3], scratch[3:]
    for dev in range(32):
        s, h = dev // 2, dev % 2
        for x in range(4):
            row = (s * 16 + x * 4 + h * 2) * 8
            put_rows(cols, row, piece_ref[dev, 2 * x : 2 * x + 2].astype(F32).reshape(16, DB))
    for a in range(8):
        grad = take_position(cols, a)
        grad_ref[a] = grad
        put_position(result, a, t_dot(f2_ref[a], grad))
    write_blocks(result, out_ref)


def write_blocks(result, out_ref):
    for dev in range(32):
        s, h = dev // 2, dev % 2
        for x in range(4):
            row = (s * 16 + x * 4 + h * 2) * 8
            value = jnp.concatenate([ref[row : row + 16, :] for ref in result], axis=1)
            out_ref[dev, 2 * x : 2 * x + 2] = value.reshape(2, 8, DB).astype(BF)


def gating_kernel(s_ref, own_ref, got_ref, second_ref, win_ref, in_ref, resid_ref, pgate_ref, sum_ref):
    zh = s_ref[0]
    own, got = own_ref[...], got_ref[...]
    first_half = jnp.where(zh == 0, own, got)
    second_half = jnp.where(zh == 0, got, own)
    value = jnp.transpose(jnp.concatenate([first_half, second_half], axis=0))
    in_ref[...] = value
    pgate = dot(value, win_ref[...]).astype(BF)
    pgate_ref[...] = pgate
    value_f = value.astype(F32)
    silu_in = value_f * jax.nn.sigmoid(value_f)
    resid = (value_f + read_pieces(second_ref) * pgate.astype(F32) * silu_in).astype(BF)
    resid_ref[...] = resid
    resid_f = resid.astype(F32)

    @pl.when(pl.program_id(0) == 0)
    def _():
        sum_ref[...] = jnp.zeros_like(sum_ref)

    put_row(sum_ref, pl.program_id(0), row_sums(resid_f * resid_f))


def mlp_kernel(s_ref, resid_ref, gain_ref, wg_ref, wu_ref, wd_ref, *refs):
    squares, cots = refs[:4], refs[4:8]
    cot_ref, normed_ref, hidden_ref, grads_ref, gnormed_ref, inner_ref = refs[8:14]
    mixed_refs = refs[14:18]
    step = pl.program_id(0)
    chunk = lax.rem(s_ref[1] + step, 4)
    for j in range(4):

        @pl.when(step == j)
        def _(j=j):
            cot_ref[...] = cots[j][...]

    cot = cot_ref[...]
    resid_f = resid_ref[...].astype(F32)
    rstd = as_column(lax.rsqrt(row_of(squares, chunk) * (1.0 / D) + 1e-06))
    gain = gain_ref[...]
    scaled_resid = resid_f * rstd
    normed = (scaled_resid * gain).astype(BF)
    normed_ref[...] = normed
    gate = dot(normed, wg_ref[...])
    upper = dot(normed, wu_ref[...])
    g_hidden = dot_t(cot, wd_ref[...])
    sig = jax.nn.sigmoid(gate)
    act = gate * sig
    hidden = (act * upper).astype(BF)
    hidden_ref[...] = hidden
    g_gate = (g_hidden * upper * sig * (1.0 + gate * (1.0 - sig))).astype(BF)
    g_up = (g_hidden * act).astype(BF)
    grads_ref[:, :768] = g_gate
    grads_ref[:, 768:] = g_up
    mixed = (resid_f + dot(hidden, wd_ref[...])).astype(BF)
    for j in range(4):

        @pl.when(step == j)
        def _(j=j):
            mixed_refs[j][...] = mixed

    g_normed = dot_t(g_gate, wg_ref[...]) + dot_t(g_up, wu_ref[...])
    gnormed_ref[...] = g_normed

    @pl.when(step == 0)
    def _():
        inner_ref[...] = jnp.zeros_like(inner_ref)

    put_row(inner_ref, chunk, row_sums(g_normed * gain * resid_f))
    inner_ref[4:5, :DB] += jnp.sum(g_normed * scaled_resid, axis=0, keepdims=True)


def resid_grad_kernel(
    _, resid_ref, cot_ref, gain_ref, gnormed_ref, in_ref, pgate_ref, *refs
):
    squares, inners, (g_resid_ref, g_second_ref) = refs[:4], refs[4:8], refs[8:]
    step = pl.program_id(0)
    rstd_row = lax.rsqrt(row_of(squares, step) * (1.0 / D) + 1e-06)
    rstd = as_column(rstd_row)
    factor = as_column(rstd_row * rstd_row * rstd_row * (row_of(inners, step) * (1.0 / D)))
    scaled = gnormed_ref[...] * gain_ref[...]
    g_resid = (
        cot_ref[...].astype(F32) + rstd * scaled - resid_ref[...].astype(F32) * factor
    ).astype(BF)
    g_resid_ref[...] = g_resid
    value = in_ref[...].astype(F32)
    silu_in = value * jax.nn.sigmoid(value)
    g_second = (g_resid.astype(F32) * pgate_ref[...].astype(F32) * silu_in).astype(BF)
    for r in range(2):
        g_second_ref[:, r] = g_second[r * 256 : (r + 1) * 256].reshape(32, 8, DB)


def direct_kernel(_, g_resid_ref, in_ref, second_ref, pgate_ref, win_ref, g_direct_ref, term_ref):
    resid_grad = g_resid_ref[...].astype(F32)
    value = in_ref[...].astype(F32)
    sig = jax.nn.sigmoid(value)
    second = read_pieces(second_ref)
    g_pgate = (resid_grad * second * (value * sig)).astype(BF)
    slope = sig * (1.0 + value * (1.0 - sig))
    through = dot_t(g_pgate, win_ref[...])
    g_direct_ref[...] = jnp.transpose(
        (resid_grad * (1.0 + second * pgate_ref[...].astype(F32) * slope) + through).astype(BF)
    )
    term = t_dot(in_ref[...], g_pgate)

    @pl.when(pl.program_id(0) == 0)
    def _():
        term_ref[...] = jnp.zeros_like(term_ref)

    term_ref[...] += term


def put_terms(s_ref, term, scratch, refs, slot):
    scratch[...] = term * (1.0 / math.sqrt(D))
    for j in range(4):
        start = pl.multiple_of(lax.rem(s_ref[1] + j, 4) * 64, 64)
        refs[j][slot] = scratch[pl.ds(start, 64), :].astype(BF)


def term_two_kernel(s_ref, grad_ref, first_ref, *refs):
    for a in range(2):
        put_terms(s_ref, dot_t(grad_ref[a], first_ref[a]), refs[4], refs[:4], a)


def term_one_kernel(s_ref, g_first_ref, in_ref, *refs):
    for r in range(2):
        g_first = g_first_ref[:, r].reshape(256, DB)
        term = dot_t(g_first, in_ref[r * 256 : (r + 1) * 256])
        put_terms(s_ref, term, refs[4], refs[:4], r)


def factor_sum_kernel(s_ref, a_ref, b_ref, c_ref, d_ref, own_ref, give_ref):
    zh = s_ref[0]
    total = (
        a_ref[...].astype(F32) + b_ref[...].astype(F32)
        + c_ref[...].astype(F32) + d_ref[...].astype(F32)
    )
    low, high = total[:, :32], total[:, 32:]
    own_ref[...] = jnp.where(zh == 0, low, high)
    give_ref[...] = jnp.where(zh == 0, high, low).astype(BF)


def factor_join_kernel(s_ref, own_ref, got_ref, out_ref):
    zh = s_ref[0]
    own, got = own_ref[...], got_ref[...].astype(F32)
    out_ref[:, 0] = jnp.where(zh == 0, own, got)
    out_ref[:, 1] = jnp.where(zh == 0, got, own)


def back_kernel(s_ref, g_first_ref, f1_ref, direct_ref, own_ref, give_ref):
    zh = s_ref[0]
    for r in range(2):
        here = slice(r * 256, (r + 1) * 256)
        back = t_dot(g_first_ref[:, r].reshape(256, DB), f1_ref[0, r])
        total = direct_ref[:, here].astype(F32) + back
        low, high = total[:192], total[192:]
        own_ref[:, here] = jnp.where(zh == 0, low, high).astype(BF)
        give_ref[:, here] = jnp.where(zh == 0, high, low).astype(BF)


def join_kernel(s_ref, own_ref, got_ref, out_ref):
    zh = s_ref[0]
    own, got = own_ref[...], got_ref[...]
    out_ref[:, :512] = jnp.where(zh == 0, own, got)
    out_ref[:, 512:] = jnp.where(zh == 0, got, own)


def mixed_join_kernel(s_ref, *refs):
    for j in range(4):
        start = pl.multiple_of(lax.rem(s_ref[1] + 4 - j, 4) * DB, DB)
        refs[4][:, pl.ds(start, DB)] = refs[j][...]


def payload_kernel(_, wg_ref, wu_ref, win_ref, wd_ref, out_ref):
    down = wd_ref[...].astype(F32)
    out_ref[:, :768] = wg_ref[...]
    out_ref[:, 768:1536] = wu_ref[...]
    out_ref[:, 1536:1920] = win_ref[...]
    out_ref[:, 1920:2304] = down[:12].astype(BF)
    out_ref[:, 2304:] = down[12:].astype(BF)


def gather_kernel(_, *refs):
    for j in range(4):
        refs[4][:, j * 512 : (j + 1) * 512] = refs[j][...]


def stack_kernel(_, *refs):
    for j in range(4):

        @pl.when(pl.program_id(0) == j)
        def _(j=j):
            refs[4][...] = refs[j][...]


def weights_kernel(s_ref, own_ref, across_ref, wg_ref, wu_ref, win_ref, wd_ref, half, down):
    mine = pl.program_id(0) == s_ref[4]
    for shard in range(16):
        value = jnp.where(mine, own_ref[shard], across_ref[shard]).astype(F32)
        half[shard * 12 : shard * 12 + 12, :] = value[:, :1920]
        down[shard * 24 : shard * 24 + 12, :] = value[:, 1920:2304]
        down[shard * 24 + 12 : shard * 24 + 24, :] = value[:, 2304:]
    wg_ref[...] = half[:, :768].astype(BF)
    wu_ref[...] = half[:, 768:1536].astype(BF)
    win_ref[...] = half[:, 1536:].astype(BF)
    wd_ref[...] = down[...].astype(BF)


def weight_grad_kernel(
    s_ref, normed_ref, grads_ref, hidden_ref, cot_ref, entry_ref, gain_ref, keep_ref, give_ref,
    across, down,
):
    step = pl.program_id(0)

    @pl.when(step == 0)
    def _():
        across[...] = jnp.zeros_like(across)
        down[...] = jnp.zeros_like(down)

    across[...] += t_dot(normed_ref[...], grads_ref[...])
    down[...] += t_dot(hidden_ref[...], cot_ref[...])

    @pl.when(step == pl.num_programs(0) - 1)
    def _():
        for ref, core in ((keep_ref, s_ref[4]), (give_ref, 1 - s_ref[4])):
            start = pl.multiple_of(core * 192, 192)
            start_down = pl.multiple_of(core * 384, 384)
            gates = across[pl.ds(start, 192), :]
            entries = entry_ref[pl.ds(start, 192), :]
            downs = down[pl.ds(start_down, 384), :]
            for shard in range(16):
                here = slice(shard * 12, shard * 12 + 12)
                at = shard * 24
                block = jnp.concatenate(
                    [gates[here], entries[here], downs[at : at + 12], downs[at + 12 : at + 24]],
                    axis=1,
                )
                ref[shard] = jnp.concatenate([block, gain_ref[...]], axis=0).astype(BF)


def pair_kernel(_, a_ref, b_ref, out_ref):
    out_ref[...] = (a_ref[...].astype(F32) + b_ref[...].astype(F32)).astype(BF)


def turn(axis, size, step):
    return [(i, (i + step) % size) for i in range(size)]


def around(value, axis):
    return [value] + [lax.ppermute(value, axis, turn(axis, 4, -j)) for j in (1, 2, 3)]


def in_order(parts, me):
    size = parts[0].shape[0]
    return lax.dynamic_slice_in_dim(
        jnp.concatenate(parts + parts, axis=0), lax.rem(4 - me, 4) * size, 4 * size, 0
    )


def send_each(parts, axis):
    return [parts[0]] + [lax.ppermute(parts[j], axis, turn(axis, 4, j)) for j in (1, 2, 3)]


Z_RING = ("zl", "zh")


def per_device(
    inputs, factor_one, factor_two, w_input_gate, norm_gain, w_gate, w_up, w_down, grad_out
):
    tok_scale = 1.0 / math.sqrt(SEQL)
    zh = lax.axis_index("zh")
    xi = lax.axis_index("x")
    yi = lax.axis_index("y")
    core = lax.axis_index("core")
    zi = lax.axis_index("zl") * 2 + zh
    at = jnp.stack([zh, xi, yi, zi, core]).astype(jnp.int32)
    bf = lambda *shape: jax.ShapeDtypeStruct(shape, BF)
    f32 = lambda *shape: jax.ShapeDtypeStruct(shape, F32)
    turned_in = inputs.T

    give = call(
        gather_kernel, (1,),
        [pl.BlockSpec((192, 512), lambda t, s, q=q: (0, 2 * q + 1 - s[0])) for q in range(4)],
        whole(192, 2048), bf(192, 2048), (1, 1),
    )(at, *[turned_in] * 4)
    other = lax.ppermute(give, "zh", SWAP)

    payload = call(
        payload_kernel, (1,),
        [whole(12, 768), whole(12, 768), whole(12, DB), whole(24, DB)],
        whole(12, 2688), bf(12, 2688), (1, 1),
    )(at, w_gate, w_up, w_input_gate, w_down)
    payload = lax.ppermute(payload, ALL, shard_moves())
    payload = jnp.broadcast_to(payload, (16, 12, 2688))
    payload, turned_in = lax.optimization_barrier((payload, turned_in))
    payload = lax.all_to_all(payload, ("zl", "y", "zh"), split_axis=0, concat_axis=0, tiled=True)

    first_local = call(
        first_kernel, (8,),
        [pl.BlockSpec((2, 256, 256), lambda t, s: (t, 0, 0)), columns(192)],
        pl.BlockSpec((32, 1, 8, DB), lambda t, s: (0, t, 0, 0)),
        bf(32, 8, 8, DB),
        (12_000_000_000, 6_000_000),
    )(at, factor_one, turned_in)
    first_local, other, payload, turned_in, grad_out, factor_two = lax.optimization_barrier(
        (first_local, other, payload, turned_in, grad_out, factor_two)
    )
    piece = lax.all_to_all(first_local, PLANE, split_axis=0, concat_axis=0, tiled=True)
    across = lax.ppermute(payload, "core", SWAP)
    wg, wu, win, wd = call(
        weights_kernel, (2,), [whole(16, 12, 2688)] * 2,
        [rows(768, 192), rows(768, 192), rows(DB, 192), rows(DB, 384)],
        [bf(DB, 768), bf(DB, 768), bf(DB, DB), bf(768, DB)], (1, 1),
        [pltpu.VMEM((192, 1920), F32), pltpu.VMEM((384, DB), F32)],
    )(at, payload, across)
    gain = lax.dynamic_slice_in_dim(norm_gain, xi * DB, DB, 0).reshape(1, DB)

    to_send = call(
        copy_three_kernel, (1,),
        [pl.BlockSpec((512, DB), lambda t, s, j=j: (0, lax.rem(s[1] + 4 - j, 4))) for j in (1, 2, 3)],
        [whole(512, DB)] * 3, [bf(512, DB)] * 3, (1, 1),
    )(at, grad_out, grad_out, grad_out)
    cots = [lax.ppermute(to_send[j - 1], "x", turn("x", 4, -j)) for j in (1, 2, 3)]
    f2 = lax.dynamic_slice_in_dim(factor_two, zh * 8, 8, 0)

    wide = [pltpu.VMEM((2048, 128), F32)] * 6
    all_pieces = whole(32, 8, 8, DB)
    second_cols, first_cols = call(
        second_kernel, (1,),
        [all_pieces, whole(8, 256, 256)],
        [all_pieces, whole(8, 256, DB)],
        [bf(32, 8, 8, DB), bf(8, 256, DB)],
        (400_000_000, 6_000_000), wide,
    )(at, piece, f2)
    second = lax.all_to_all(second_cols, PLANE, split_axis=0, concat_axis=0, tiled=True)

    input_mlp, resid, pgate, square = call(
        gating_kernel, (4,),
        [pl.BlockSpec((192, 512), lambda t, s: (0, 2 * t + s[0])), columns(192), PIECES, whole(DB, DB)],
        [rows(DB), rows(DB), rows(DB), whole(8, 512)],
        [bf(2048, DB), bf(2048, DB), bf(2048, DB), f32(8, 512)],
        (600_000_000, 10_000_000),
    )(at, turned_in, other, second, win)
    squares = around(square, "x")
    own_cot = pl.BlockSpec((512, DB), lambda t, s: (0, s[1]))
    cot, normed, hidden, grads, g_normed, inner, *mixed = call(
        mlp_kernel, (4,),
        [turned_rows(DB), whole(1, DB), whole(DB, 768), whole(DB, 768), whole(768, DB)]
        + SUMS + [own_cot] + [whole(512, DB)] * 3,
        [turned_rows(DB), turned_rows(DB), turned_rows(768), turned_rows(1536), turned_rows(DB), whole(8, 512)]
        + [whole(512, DB)] * 4,
        [bf(2048, DB), bf(2048, DB), bf(2048, 768), bf(2048, 1536), f32(2048, DB), f32(8, 512)]
        + [bf(512, DB)] * 4,
        (7_300_000_000, 24_000_000),
    )(at, resid, gain, wg, wu, wd, *squares, grad_out, *cots)
    inners = around(inner, "x")
    g_resid, g_second = call(
        resid_grad_kernel, (4,),
        [rows(DB), rows(DB), whole(1, DB), rows(DB), rows(DB), rows(DB)] + SUMS + SUMS,
        [rows(DB), PIECES],
        [bf(2048, DB), bf(32, 8, 8, DB)],
        (50_000_000, 12_000_000),
    )(at, resid, cot, gain, g_normed, input_mlp, pgate, *squares, *inners)
    g_second, normed, hidden, grads, cot, mixed, inners = lax.optimization_barrier(
        (g_second, normed, hidden, grads, cot, mixed, inners)
    )
    piece = lax.all_to_all(g_second, PLANE, split_axis=0, concat_axis=0, tiled=True)

    mixed = send_each(mixed, "x")
    mixed_out = call(
        mixed_join_kernel, (1,), [whole(512, DB)] * 4, whole(512, D),
        bf(512, D), (1, 1),
    )(at, *mixed)
    g_direct, term_entry = call(
        direct_kernel, (4,),
        [rows(DB), rows(DB), PIECES, rows(DB), whole(DB, DB)],
        [columns(DB), whole(DB, DB)],
        [bf(DB, 2048), f32(DB, DB)],
        (1, 1),
    )(at, g_resid, input_mlp, second, pgate, win)

    gain_terms = in_order([v[4:5, :DB] for v in inners], xi).reshape(1, D)
    gain_rows = jnp.pad(gain_terms, ((0, 3), (0, 2688 - D)))
    shards = whole(16, 16, 2688)
    keep, give = call(
        weight_grad_kernel, (4,),
        [rows(DB), rows(1536), rows(768), rows(DB), whole(DB, DB), whole(4, 2688)],
        [shards] * 2, [bf(16, 16, 2688)] * 2, (1, 1),
        [pltpu.VMEM((DB, 1536), F32), pltpu.VMEM((768, DB), F32)],
    )(at, normed, grads, hidden, cot, term_entry, gain_rows)
    got = lax.ppermute(give, "core", SWAP)
    quarter = pl.BlockSpec((8, 16, 2688), lambda t, s: (t, 0, 0))
    pair = call(pair_kernel, (2,), [quarter] * 2, quarter, bf(16, 16, 2688), (1, 1))(at, keep, got)

    piece, pair = lax.optimization_barrier((piece, pair))
    pair = lax.all_to_all(pair, ("zl", "y", "zh"), split_axis=0, concat_axis=0, tiled=True)

    first_grad, second_grad = call(
        first_grad_kernel, (1,),
        [all_pieces, whole(8, 256, 256)],
        [all_pieces, whole(8, 256, DB)],
        [bf(32, 8, 8, DB), bf(8, 256, DB)],
        (400_000_000, 6_000_000), wide,
    )(at, piece, f2)
    square_scratch = [pltpu.VMEM((256, 256), F32)]
    term_out = pl.BlockSpec((2, 64, 256), lambda t, s: (t, 0, 0))

    terms_two = call(
        term_two_kernel, (4,),
        [pl.BlockSpec((2, 256, DB), lambda t, s: (t, 0, 0))] * 2,
        [term_out] * 4, [bf(8, 64, 256)] * 4, (1, 1), square_scratch,
    )(at, second_grad, first_cols)
    first_grad, terms_two, pair, mixed_out = lax.optimization_barrier(
        (first_grad, terms_two, pair, mixed_out)
    )
    g_first = lax.all_to_all(first_grad, PLANE, split_axis=0, concat_axis=0, tiled=True)

    def factor_sums(terms):
        return call(
            factor_sum_kernel, (1,), [whole(8, 64, 256)] * 4, [whole(8, 32, 256)] * 2,
            [f32(8, 32, 256), bf(8, 32, 256)], (1, 1),
        )(at, *send_each(terms, "x"))

    def factor_gradient(sums, slots):
        own, give = sums
        got = lax.ppermute(give, "zh", SWAP)
        shape = (slots, 8 // slots, 32, 256)
        joined = call(
            factor_join_kernel, (1,), [whole(*shape)] * 2, whole(slots, 2, 8 // slots, 32, 256),
            f32(slots, 2, 8 // slots, 32, 256), (1, 1),
        )(at, own.reshape(shape), got.reshape(shape))
        return joined.reshape(16, 32, 256)

    sums_two = factor_sums(terms_two)

    summed = jnp.sum(pair.astype(F32), axis=0) * tok_scale
    back = [(there, here) for here, there in shard_moves()]
    own = lax.ppermute(summed[:12], ALL, back)
    g_first, own, sums_two = lax.optimization_barrier((g_first, own, sums_two))
    grad_w_gate, grad_w_up = own[:, :768], own[:, 768:1536]
    grad_w_input_gate = own[:, 1536:1920]
    grad_w_down = jnp.concatenate([own[:, 1920:2304], own[:, 2304:]], axis=0)
    grad_norm_gain = summed[12, :D]
    grad_factor_two = factor_gradient(sums_two, 1)

    own_grad, give_grad = call(
        back_kernel, (4,),
        [PIECES, pl.BlockSpec((1, 2, 256, 256), lambda t, s: (2 * t + s[0], 0, 0, 0)), columns(DB)],
        [columns(192), columns(192)],
        [bf(192, 2048), bf(192, 2048)],
        (400_000_000, 6_000_000),
    )(at, g_first, factor_one.reshape(8, 2, 256, 256), g_direct)
    g_first, give_grad = lax.optimization_barrier((g_first, give_grad))
    terms_one = call(
        term_one_kernel, (4,), [PIECES, rows(DB)],
        [term_out] * 4, [bf(8, 64, 256)] * 4, (1, 1), square_scratch,
    )(at, g_first, input_mlp)
    grad_factor_one = factor_gradient(factor_sums(terms_one), 4)

    got_grad = lax.ppermute(give_grad, "zh", SWAP)
    grad_inputs = call(
        join_kernel, (4,), [columns(192), columns(192)], columns(192, 1024), bf(192, 4096), (1, 1)
    )(at, own_grad, got_grad).T
    return (
        mixed_out,
        grad_inputs,
        grad_factor_one,
        grad_factor_two,
        grad_w_input_gate,
        grad_norm_gain,
        grad_w_gate,
        grad_w_up,
        grad_w_down,
    )


def solution(mesh):
    fine = Mesh(mesh.devices.reshape(SIZES), ALL)
    return jax.shard_map(
        per_device,
        mesh=fine,
        in_specs=(
            P(SEQ, CH),
            P(SEQ, None, None),
            P(SEQ, None, None),
            P(ALL, None),
            P(),
            P(ALL, None),
            P(ALL, None),
            P(ALL, None),
            P(ALL, None),
        ),
        out_specs=(
            P(ALL, None),
            P(SEQ, CH),
            P(SEQ, CH, None),
            P(SEQ, CH, None),
            P(ALL, None),
            P(),
            P(ALL, None),
            P(ALL, None),
            P(ALL, None),
        ),
        check_vma=False,
    )
```

```python
import math

import jax
import jax.numpy as jnp
from jax import lax
from jax.experimental import pallas as pl
from jax.experimental.pallas import tpu as pltpu
from jax.sharding import Mesh
from jax.sharding import PartitionSpec as P

D = 1536
NBLK = 4
SEQL = 65536
DB = D // NBLK
BF = jnp.bfloat16
F32 = jnp.float32

SEQ = ("zl", "y", "core")
CH = ("x", "zh")
ALL = SEQ + CH
SIZES = (2, 4, 2, 4, 2)
PLANE = SEQ + ("zh",)


def index_of(zl, y, k, x, zh):
    return (((zl * 4 + y) * 2 + k) * 4 + x) * 2 + zh


def shard_moves():
    moves = []
    for zl in range(2):
        for y in range(4):
            for k in range(2):
                for x in range(4):
                    for zh in range(2):
                        there = index_of(y % 2, k * 2 + x // 2, x % 2, zl * 2 + y // 2, zh)
                        moves.append((index_of(zl, y, k, x, zh), there))
    return moves


SWAP = [(0, 1), (1, 0)]


def call(body, grid, ins, outs, shapes, cost, scratch=()):
    return pl.pallas_call(
        body,
        grid_spec=pltpu.PrefetchScalarGridSpec(
            num_scalar_prefetch=1,
            grid=grid,
            in_specs=ins,
            out_specs=outs,
            scratch_shapes=list(scratch),
        ),
        out_shape=shapes,
        name=body.__name__,
        compiler_params=pltpu.CompilerParams(
            dimension_semantics=("arbitrary",) * len(grid), vmem_limit_bytes=56 * 1024 * 1024
        ),
        cost_estimate=pl.CostEstimate(flops=cost[0], bytes_accessed=cost[1], transcendentals=0),
    )


def whole(*shape):
    return pl.BlockSpec(shape, lambda t, s: (0,) * len(shape))


def rows(width, height=512):
    return pl.BlockSpec((height, width), lambda t, s: (t, 0))


def turned_rows(width, height=512):
    return pl.BlockSpec((height, width), lambda t, s: (lax.rem(s[1] + t, 4), 0))


def columns(height, width=512):
    return pl.BlockSpec((height, width), lambda t, s: (0, t))


PIECES = pl.BlockSpec((32, 2, 8, DB), lambda t, s: (0, t, 0, 0))
SUMS = [whole(8, 512)] * 4


def read_pieces(ref):
    return jnp.concatenate(
        [ref[:, r].astype(F32).reshape(256, DB) for r in range(2)], axis=0
    )


def row_sums(value):
    ones = jnp.ones((8, DB), BF)
    high = value.astype(BF)
    low = (value - high.astype(F32)).astype(BF)
    return dot_t(ones, high) + dot_t(ones, low)


def row_of(refs, at):
    total = refs[0][...] + refs[1][...] + refs[2][...] + refs[3][...]
    here = lax.broadcasted_iota(jnp.int32, (8, 512), 0) == at
    return jnp.sum(jnp.where(here, total, 0.0), axis=0, keepdims=True)


def put_row(ref, at, value):
    here = lax.broadcasted_iota(jnp.int32, (8, 512), 0) == at
    ref[...] = jnp.where(here, value, ref[...])


def as_column(row):
    turned = jnp.transpose(jnp.broadcast_to(row, (128, row.shape[1])))
    return jnp.concatenate([turned] * (DB // 128), axis=1)


def dot(a, b):
    return jnp.dot(a, b, preferred_element_type=F32)


def dot_t(a, b):
    return lax.dot_general(a, b, (((1,), (1,)), ((), ())), preferred_element_type=F32)


def t_dot(a, b):
    return lax.dot_general(a, b, (((0,), (0,)), ((), ())), preferred_element_type=F32)


def first_kernel(_, f1_ref, in_ref, payload_ref, out_ref):
    step = pl.program_id(0)

    @pl.when(step < 8)
    def _():
        results = [
            dot_t(f1_ref[r], in_ref[:, r * 256 : (r + 1) * 256]).reshape(32, 8, 192)
            for r in range(2)
        ]
        out_ref[:, 0] = jnp.concatenate(results, axis=2).astype(BF)

    @pl.when(step >= 8)
    def _():
        halves = [payload_ref[core, lax.max(step - 8, 0)] for core in range(2)]
        for dev in range(32):
            out_ref[dev, 0] = halves[dev // 2 % 2]


def copy_kernel(_, in_ref, out_ref):
    out_ref[...] = in_ref[...]


def copy_three_kernel(_, *refs):
    for j in range(3):
        refs[3 + j][...] = refs[j][...]


def put_rows(refs, row, value):
    for j, ref in enumerate(refs):
        ref[row : row + value.shape[0], :] = value[:, j * 128 : (j + 1) * 128]


def put_position(refs, a, value):
    for j, ref in enumerate(refs):
        ref[pl.ds(a, 256, stride=8), :] = value[:, j * 128 : (j + 1) * 128]


def take_position(refs, a):
    parts = [ref[pl.ds(a, 256, stride=8), :] for ref in refs]
    return jnp.concatenate(parts, axis=1).astype(BF)


def second_kernel(_, piece_ref, f2_ref, out_ref, first_ref, *scratch):
    cols, result = scratch[:3], scratch[3:]
    for s in range(16):
        for pair in range(8):
            low, high = (piece_ref[2 * s + h, pair].astype(F32) for h in range(2))
            row = (s * 16 + pair * 2) * 8
            put_rows(cols, row, jnp.concatenate([low[:, :192], high[:, :192]], axis=1))
            put_rows(cols, row + 8, jnp.concatenate([low[:, 192:], high[:, 192:]], axis=1))
    for a in range(8):
        first = take_position(cols, a)
        first_ref[a] = first
        put_position(result, a, dot(f2_ref[a], first))
    write_blocks(result, out_ref)


def first_grad_kernel(_, piece_ref, f2_ref, keep_ref, got_ref, out_ref, grad_ref, *scratch):
    cols, result = scratch[:3], scratch[3:]
    for dev in range(32):
        s, h = dev // 2, dev % 2
        for x in range(4):
            row = (s * 16 + x * 4 + h * 2) * 8
            put_rows(cols, row, piece_ref[dev, 2 * x : 2 * x + 2].astype(F32).reshape(16, DB))
    for a in range(8):
        grad = take_position(cols, a)
        grad_ref[a] = grad
        put_position(result, a, t_dot(f2_ref[a], grad))
    write_blocks(result, out_ref)
    for dev in range(32):
        total = keep_ref[dev].astype(F32) + got_ref[dev].astype(F32)
        out_ref[dev, 8:] = total.astype(BF)


def write_blocks(result, out_ref):
    for dev in range(32):
        s, h = dev // 2, dev % 2
        for x in range(4):
            row = (s * 16 + x * 4 + h * 2) * 8
            value = jnp.concatenate([ref[row : row + 16, :] for ref in result], axis=1)
            out_ref[dev, 2 * x : 2 * x + 2] = value.reshape(2, 8, DB).astype(BF)


def gating_kernel(s_ref, own_ref, got_ref, second_ref, win_ref, in_ref, resid_ref, pgate_ref, sum_ref):
    zh = s_ref[0]
    own, got = own_ref[...], got_ref[...]
    first_half = jnp.where(zh == 0, own, got)
    second_half = jnp.where(zh == 0, got, own)
    value = jnp.transpose(jnp.concatenate([first_half, second_half], axis=0))
    in_ref[...] = value
    pgate = dot(value, win_ref[...]).astype(BF)
    pgate_ref[...] = pgate
    value_f = value.astype(F32)
    silu_in = value_f * jax.nn.sigmoid(value_f)
    resid = (value_f + read_pieces(second_ref) * pgate.astype(F32) * silu_in).astype(BF)
    resid_ref[...] = resid
    resid_f = resid.astype(F32)

    @pl.when(pl.program_id(0) == 0)
    def _():
        sum_ref[...] = jnp.zeros_like(sum_ref)

    put_row(sum_ref, pl.program_id(0), row_sums(resid_f * resid_f))


def mlp_kernel(s_ref, resid_ref, gain_ref, wg_ref, wu_ref, wd_ref, *refs):
    squares, cots = refs[:4], refs[4:8]
    cot_ref, normed_ref, hidden_ref, grads_ref, gnormed_ref, inner_ref = refs[8:14]
    mixed_refs = refs[14:18]
    step = pl.program_id(0)
    chunk = lax.rem(s_ref[1] + step, 4)
    for j in range(4):

        @pl.when(step == j)
        def _(j=j):
            cot_ref[...] = cots[j][...]

    cot = cot_ref[...]
    resid_f = resid_ref[...].astype(F32)
    rstd = as_column(lax.rsqrt(row_of(squares, chunk) * (1.0 / D) + 1e-06))
    gain = gain_ref[...]
    scaled_resid = resid_f * rstd
    normed = (scaled_resid * gain).astype(BF)
    normed_ref[...] = normed
    gate = dot(normed, wg_ref[...])
    upper = dot(normed, wu_ref[...])
    g_hidden = dot_t(cot, wd_ref[...])
    sig = jax.nn.sigmoid(gate)
    act = gate * sig
    hidden = (act * upper).astype(BF)
    hidden_ref[...] = hidden
    g_gate = (g_hidden * upper * sig * (1.0 + gate * (1.0 - sig))).astype(BF)
    g_up = (g_hidden * act).astype(BF)
    grads_ref[:, :768] = g_gate
    grads_ref[:, 768:] = g_up
    mixed = (resid_f + dot(hidden, wd_ref[...])).astype(BF)
    for j in range(4):

        @pl.when(step == j)
        def _(j=j):
            mixed_refs[j][...] = mixed

    g_normed = dot_t(g_gate, wg_ref[...]) + dot_t(g_up, wu_ref[...])
    gnormed_ref[...] = g_normed

    @pl.when(step == 0)
    def _():
        inner_ref[...] = jnp.zeros_like(inner_ref)

    put_row(inner_ref, chunk, row_sums(g_normed * gain * resid_f))
    inner_ref[4:5, :DB] += jnp.sum(g_normed * scaled_resid, axis=0, keepdims=True)


def resid_grad_kernel(
    _, resid_ref, cot_ref, gain_ref, gnormed_ref, in_ref, pgate_ref, *refs
):
    squares, inners, (g_resid_ref, g_second_ref) = refs[:4], refs[4:8], refs[8:]
    step = pl.program_id(0)
    rstd_row = lax.rsqrt(row_of(squares, step) * (1.0 / D) + 1e-06)
    rstd = as_column(rstd_row)
    factor = as_column(rstd_row * rstd_row * rstd_row * (row_of(inners, step) * (1.0 / D)))
    scaled = gnormed_ref[...] * gain_ref[...]
    g_resid = (
        cot_ref[...].astype(F32) + rstd * scaled - resid_ref[...].astype(F32) * factor
    ).astype(BF)
    g_resid_ref[...] = g_resid
    value = in_ref[...].astype(F32)
    silu_in = value * jax.nn.sigmoid(value)
    g_second = (g_resid.astype(F32) * pgate_ref[...].astype(F32) * silu_in).astype(BF)
    for r in range(2):
        g_second_ref[:, r] = g_second[r * 256 : (r + 1) * 256].reshape(32, 8, DB)


def direct_kernel(_, g_resid_ref, in_ref, second_ref, pgate_ref, win_ref, g_direct_ref, term_ref):
    resid_grad = g_resid_ref[...].astype(F32)
    value = in_ref[...].astype(F32)
    sig = jax.nn.sigmoid(value)
    second = read_pieces(second_ref)
    g_pgate = (resid_grad * second * (value * sig)).astype(BF)
    slope = sig * (1.0 + value * (1.0 - sig))
    through = dot_t(g_pgate, win_ref[...])
    g_direct_ref[...] = jnp.transpose(
        (resid_grad * (1.0 + second * pgate_ref[...].astype(F32) * slope) + through).astype(BF)
    )
    term = t_dot(in_ref[...], g_pgate)

    @pl.when(pl.program_id(0) == 0)
    def _():
        term_ref[...] = jnp.zeros_like(term_ref)

    term_ref[...] += term


def put_terms(s_ref, term, scratch, refs, slot):
    scratch[...] = term * (1.0 / math.sqrt(D))
    for j in range(4):
        start = pl.multiple_of(lax.rem(s_ref[1] + j, 4) * 64, 64)
        refs[j][slot] = scratch[pl.ds(start, 64), :].astype(BF)


def term_two_kernel(s_ref, grad_ref, first_ref, *refs):
    for a in range(2):
        put_terms(s_ref, dot_t(grad_ref[a], first_ref[a]), refs[4], refs[:4], a)


def term_one_kernel(s_ref, g_first_ref, in_ref, *refs):
    for r in range(2):
        g_first = g_first_ref[:, r].reshape(256, DB)
        term = dot_t(g_first, in_ref[r * 256 : (r + 1) * 256])
        put_terms(s_ref, term, refs[4], refs[:4], r)


def factor_sum_kernel(s_ref, a_ref, b_ref, c_ref, d_ref, own_ref, give_ref):
    zh = s_ref[0]
    total = (
        a_ref[...].astype(F32) + b_ref[...].astype(F32)
        + c_ref[...].astype(F32) + d_ref[...].astype(F32)
    )
    low, high = total[:, :32], total[:, 32:]
    own_ref[...] = jnp.where(zh == 0, low, high)
    give_ref[...] = jnp.where(zh == 0, high, low).astype(BF)


def factor_join_kernel(s_ref, own_ref, got_ref, out_ref):
    zh = s_ref[0]
    own, got = own_ref[...], got_ref[...].astype(F32)
    out_ref[:, 0] = jnp.where(zh == 0, own, got)
    out_ref[:, 1] = jnp.where(zh == 0, got, own)


def back_kernel(s_ref, g_first_ref, f1_ref, direct_ref, own_ref, give_ref):
    zh = s_ref[0]
    for r in range(2):
        here = slice(r * 256, (r + 1) * 256)
        back = t_dot(g_first_ref[:, r].reshape(256, DB), f1_ref[0, r])
        total = direct_ref[:, here].astype(F32) + back
        low, high = total[:192], total[192:]
        own_ref[:, here] = jnp.where(zh == 0, low, high).astype(BF)
        give_ref[:, here] = jnp.where(zh == 0, high, low).astype(BF)


def join_kernel(s_ref, own_ref, got_ref, out_ref):
    zh = s_ref[0]
    for q in range(2):
        here = slice(q * 512, (q + 1) * 512)
        own, got = own_ref[:, here], got_ref[:, here]
        out_ref[:, q * 1024 : q * 1024 + 512] = jnp.where(zh == 0, own, got)
        out_ref[:, q * 1024 + 512 : (q + 1) * 1024] = jnp.where(zh == 0, got, own)


def mixed_join_kernel(s_ref, *refs):
    for j in range(4):
        start = pl.multiple_of(lax.rem(s_ref[1] + 4 - j, 4) * DB, DB)
        refs[4][:, pl.ds(start, DB)] = refs[j][...]


def payload_kernel(_, wg_ref, wu_ref, win_ref, wd_ref, out_ref):
    wg, wu = wg_ref[...].astype(F32), wu_ref[...].astype(F32)
    win, down = win_ref[...].astype(F32), wd_ref[...].astype(F32)
    put_half(out_ref, 0, [wg[:, :DB], wg[:, DB:], win, jnp.zeros_like(win)])
    put_half(out_ref, 1, [wu[:, :DB], wu[:, DB:], down])


def put_half(ref, at, parts):
    ref[at] = jnp.concatenate(parts, axis=0).reshape(6, 8, DB).astype(BF)


def gather_kernel(_, *refs):
    for j in range(4):
        refs[4][:, j * 512 : (j + 1) * 512] = refs[j][...]


def weights_kernel(s_ref, own_ref, across_ref, wg_ref, wu_ref, win_ref, wd_ref):
    first = s_ref[4] == 0
    gates, ups, entries, downs = [], [], [], []
    for shard in range(8):
        own = own_ref[shard].astype(F32).reshape(48, DB)
        across = across_ref[shard].astype(F32).reshape(48, DB)
        low, high = jnp.where(first, own, across), jnp.where(first, across, own)
        gates.append(jnp.concatenate([low[:12], low[12:24]], axis=1))
        entries.append(low[24:36])
        ups.append(jnp.concatenate([high[:12], high[12:24]], axis=1))
        downs.append(high[24:])
    for ref, parts in ((wg_ref, gates), (wu_ref, ups), (win_ref, entries), (wd_ref, downs)):
        ref[...] = jnp.concatenate(parts, axis=0).astype(BF)


def weight_grad_kernel(
    s_ref, normed_ref, grads_ref, hidden_ref, cot_ref, entry_ref, gain_ref, keep_ref, give_ref,
    across, down,
):
    step = pl.program_id(0)

    @pl.when(step == 0)
    def _():
        across[...] = jnp.zeros_like(across)
        down[...] = jnp.zeros_like(down)

    across[...] += t_dot(normed_ref[...], grads_ref[...])
    down[...] += t_dot(hidden_ref[...], cot_ref[...])

    @pl.when(step == pl.num_programs(0) - 1)
    def _():
        first = s_ref[4] == 0
        fill = jnp.zeros((8, DB), F32)
        for shard in range(32):
            here = slice(shard * 12, shard * 12 + 12)
            gates, entries = across[here, :], entry_ref[here, :]
            low = [gates[:, :DB], gates[:, DB : 2 * DB], entries, gain_ref[...], fill]
            high = [gates[:, 2 * DB : 3 * DB], gates[:, 3 * DB :]]
            high.append(down[shard * 24 : shard * 24 + 24, :])
            low = jnp.concatenate(low, axis=0)
            high = jnp.concatenate(high, axis=0)
            put_half(keep_ref, shard, [jnp.where(first, low, high)])
            put_half(give_ref, shard, [jnp.where(first, high, low)])


def weight_sum_kernel(_, in_ref, out_ref):
    for core in range(2):
        total = jnp.zeros((2, 8, DB), F32)
        for pair in range(8):
            for zh in range(2):
                total = total + in_ref[pair * 4 + core * 2 + zh].astype(F32)
        out_ref[core] = total * (1.0 / math.sqrt(SEQL))


def turn(axis, size, step):
    return [(i, (i + step) % size) for i in range(size)]


def around(value, axis):
    return [value] + [lax.ppermute(value, axis, turn(axis, 4, -j)) for j in (1, 2, 3)]


def in_order(parts, me):
    size = parts[0].shape[0]
    return lax.dynamic_slice_in_dim(
        jnp.concatenate(parts + parts, axis=0), lax.rem(4 - me, 4) * size, 4 * size, 0
    )


def send_each(parts, axis):
    return [parts[0]] + [lax.ppermute(parts[j], axis, turn(axis, 4, j)) for j in (1, 2, 3)]


Z_RING = ("zl", "zh")


def per_device(
    inputs, factor_one, factor_two, w_input_gate, norm_gain, w_gate, w_up, w_down, grad_out
):
    tok_scale = 1.0 / math.sqrt(SEQL)
    zh = lax.axis_index("zh")
    xi = lax.axis_index("x")
    yi = lax.axis_index("y")
    core = lax.axis_index("core")
    zi = lax.axis_index("zl") * 2 + zh
    at = jnp.stack([zh, xi, yi, zi, core]).astype(jnp.int32)
    bf = lambda *shape: jax.ShapeDtypeStruct(shape, BF)
    f32 = lambda *shape: jax.ShapeDtypeStruct(shape, F32)
    turned_in = inputs.T

    give = call(
        gather_kernel, (1,),
        [pl.BlockSpec((192, 512), lambda t, s, q=q: (0, 2 * q + 1 - s[0])) for q in range(4)],
        whole(192, 2048), bf(192, 2048), (1, 1),
    )(at, *[turned_in] * 4)
    other = lax.ppermute(give, "zh", SWAP)
    give, turned_in, w_gate = lax.optimization_barrier((give, turned_in, w_gate))

    payload = call(
        payload_kernel, (1,),
        [whole(12, 768), whole(12, 768), whole(12, DB), whole(24, DB)],
        whole(2, 6, 8, DB), bf(2, 6, 8, DB), (1, 1),
    )(at, w_gate, w_up, w_input_gate, w_down)
    payload = lax.ppermute(payload, ALL, shard_moves())
    first_local = call(
        first_kernel, (14,),
        [pl.BlockSpec((2, 256, 256), lambda t, s: (lax.min(t, 7), 0, 0)),
         pl.BlockSpec((192, 512), lambda t, s: (0, lax.min(t, 7))), whole(2, 6, 8, DB)],
        pl.BlockSpec((32, 1, 8, DB), lambda t, s: (0, t, 0, 0)),
        bf(32, 14, 8, DB),
        (12_000_000_000, 6_000_000),
    )(at, factor_one, turned_in, payload)
    first_local, other, turned_in, grad_out, factor_two = lax.optimization_barrier(
        (first_local, other, turned_in, grad_out, factor_two)
    )
    piece = lax.all_to_all(first_local, PLANE, split_axis=0, concat_axis=0, tiled=True)
    gain = lax.dynamic_slice_in_dim(norm_gain, xi * DB, DB, 0).reshape(1, DB)

    to_send = call(
        copy_three_kernel, (1,),
        [pl.BlockSpec((512, DB), lambda t, s, j=j: (0, lax.rem(s[1] + 4 - j, 4))) for j in (1, 2, 3)],
        [whole(512, DB)] * 3, [bf(512, DB)] * 3, (1, 1),
    )(at, grad_out, grad_out, grad_out)
    cots = [lax.ppermute(to_send[j - 1], "x", turn("x", 4, -j)) for j in (1, 2, 3)]
    f2 = lax.dynamic_slice_in_dim(factor_two, zh * 8, 8, 0)

    wide = [pltpu.VMEM((2048, 128), F32)] * 6
    all_pieces = whole(32, 8, 8, DB)
    second_cols, first_cols = call(
        second_kernel, (1,),
        [whole(32, 14, 8, DB), whole(8, 256, 256)],
        [all_pieces, whole(8, 256, DB)],
        [bf(32, 8, 8, DB), bf(8, 256, DB)],
        (400_000_000, 6_000_000), wide,
    )(at, piece, f2)
    second_cols, piece = lax.optimization_barrier((second_cols, piece))
    second = lax.all_to_all(second_cols, PLANE, split_axis=0, concat_axis=0, tiled=True)

    half = piece[:, 8:]
    across = lax.ppermute(half, "core", SWAP)
    shards = pl.BlockSpec((8, 6, 8, DB), lambda t, s: (t, 0, 0, 0))
    wg, wu, win, wd = call(
        weights_kernel, (4,), [shards] * 2,
        [rows(768, 96), rows(768, 96), rows(DB, 96), rows(DB, 192)],
        [bf(DB, 768), bf(DB, 768), bf(DB, DB), bf(768, DB)], (1, 1),
    )(at, half, across)

    input_mlp, resid, pgate, square = call(
        gating_kernel, (4,),
        [pl.BlockSpec((192, 512), lambda t, s: (0, 2 * t + s[0])),
         columns(192), PIECES, whole(DB, DB)],
        [rows(DB), rows(DB), rows(DB), whole(8, 512)],
        [bf(2048, DB), bf(2048, DB), bf(2048, DB), f32(8, 512)],
        (600_000_000, 10_000_000),
    )(at, turned_in, other, second, win)
    squares = around(square, "x")
    own_cot = pl.BlockSpec((512, DB), lambda t, s: (0, s[1]))
    cot, normed, hidden, grads, g_normed, inner, *mixed = call(
        mlp_kernel, (4,),
        [turned_rows(DB), whole(1, DB), whole(DB, 768), whole(DB, 768), whole(768, DB)]
        + SUMS + [own_cot] + [whole(512, DB)] * 3,
        [turned_rows(DB), turned_rows(DB), turned_rows(768), turned_rows(1536), turned_rows(DB), whole(8, 512)]
        + [whole(512, DB)] * 4,
        [bf(2048, DB), bf(2048, DB), bf(2048, 768), bf(2048, 1536), f32(2048, DB), f32(8, 512)]
        + [bf(512, DB)] * 4,
        (7_300_000_000, 24_000_000),
    )(at, resid, gain, wg, wu, wd, *squares, grad_out, *cots)
    inners = around(inner, "x")
    g_resid, g_second = call(
        resid_grad_kernel, (4,),
        [rows(DB), rows(DB), whole(1, DB), rows(DB), rows(DB), rows(DB)] + SUMS + SUMS,
        [rows(DB), PIECES],
        [bf(2048, DB), bf(32, 8, 8, DB)],
        (50_000_000, 12_000_000),
    )(at, resid, cot, gain, g_normed, input_mlp, pgate, *squares, *inners)
    g_second, normed, hidden, grads, cot, mixed, inners = lax.optimization_barrier(
        (g_second, normed, hidden, grads, cot, mixed, inners)
    )
    piece = lax.all_to_all(g_second, PLANE, split_axis=0, concat_axis=0, tiled=True)

    mixed = send_each(mixed, "x")
    mixed_out = call(
        mixed_join_kernel, (1,), [whole(512, DB)] * 4, whole(512, D),
        bf(512, D), (1, 1),
    )(at, *mixed)
    g_direct, term_entry = call(
        direct_kernel, (4,),
        [rows(DB), rows(DB), PIECES, rows(DB), whole(DB, DB)],
        [columns(DB), whole(DB, DB)],
        [bf(DB, 2048), f32(DB, DB)],
        (1, 1),
    )(at, g_resid, input_mlp, second, pgate, win)

    gain_terms = in_order([v[4:5, :DB] for v in inners], xi).reshape(1, D)
    gain_rows = gain_terms.reshape(4, DB)
    halves = whole(32, 6, 8, DB)
    keep, give = call(
        weight_grad_kernel, (2,),
        [rows(DB, 1024), rows(1536, 1024), rows(768, 1024), rows(DB, 1024), whole(DB, DB), whole(4, DB)],
        [halves] * 2, [bf(32, 6, 8, DB)] * 2, (1, 1),
        [pltpu.VMEM((DB, 1536), F32), pltpu.VMEM((768, DB), F32)],
    )(at, normed, grads, hidden, cot, term_entry, gain_rows)
    got = lax.ppermute(give, "core", SWAP)

    first_grad, second_grad = call(
        first_grad_kernel, (1,),
        [all_pieces, whole(8, 256, 256), halves, halves],
        [whole(32, 14, 8, DB), whole(8, 256, DB)],
        [bf(32, 14, 8, DB), bf(8, 256, DB)],
        (400_000_000, 6_000_000), wide,
    )(at, piece, f2, keep, got)
    square_scratch = [pltpu.VMEM((256, 256), F32)]
    term_out = pl.BlockSpec((2, 64, 256), lambda t, s: (t, 0, 0))

    first_grad, second_grad = lax.optimization_barrier((first_grad, second_grad))
    g_first = lax.all_to_all(first_grad, PLANE, split_axis=0, concat_axis=0, tiled=True)

    def factor_sums(terms):
        return call(
            factor_sum_kernel, (1,), [whole(8, 64, 256)] * 4, [whole(8, 32, 256)] * 2,
            [f32(8, 32, 256), bf(8, 32, 256)], (1, 1),
        )(at, *terms)

    def factor_gradient(own, got, slots):
        shape = (slots, 8 // slots, 32, 256)
        joined = call(
            factor_join_kernel, (1,), [whole(*shape)] * 2, whole(slots, 2, 8 // slots, 32, 256),
            f32(slots, 2, 8 // slots, 32, 256), (1, 1),
        )(at, own.reshape(shape), got.reshape(shape))
        return joined.reshape(16, 32, 256)

    terms_two = call(
        term_two_kernel, (4,),
        [pl.BlockSpec((2, 256, DB), lambda t, s: (t, 0, 0))] * 2,
        [term_out] * 4, [bf(8, 64, 256)] * 4, (1, 1), square_scratch,
    )(at, second_grad, first_cols)
    sums_two = factor_sums(send_each(terms_two, "x"))

    g_first, sums_two, mixed_out = lax.optimization_barrier((g_first, sums_two, mixed_out))
    own_grad, give_grad = call(
        back_kernel, (4,),
        [PIECES, pl.BlockSpec((1, 2, 256, 256), lambda t, s: (2 * t + s[0], 0, 0, 0)), columns(DB)],
        [columns(192), columns(192)],
        [bf(192, 2048), bf(192, 2048)],
        (12_000_000_000, 6_000_000),
    )(at, g_first, factor_one.reshape(8, 2, 256, 256), g_direct)
    g_first, give_grad = lax.optimization_barrier((g_first, give_grad))
    terms_one = call(
        term_one_kernel, (4,), [PIECES, rows(DB)],
        [term_out] * 4, [bf(8, 64, 256)] * 4, (1, 1), square_scratch,
    )(at, g_first, input_mlp)

    terms_one, sums_two = lax.optimization_barrier((terms_one, sums_two))
    got_two = lax.ppermute(sums_two[1], "zh", SWAP)
    for_sums, got_two = lax.optimization_barrier((g_first, got_two))
    got_grad = lax.ppermute(give_grad, "zh", SWAP)
    summed = call(
        weight_sum_kernel, (3,),
        [pl.BlockSpec((32, 2, 8, DB), lambda t, s: (0, t + 4, 0, 0))],
        pl.BlockSpec((2, 2, 8, DB), lambda t, s: (0, t, 0, 0)), f32(2, 6, 8, DB), (1, 1),
    )(at, for_sums)
    back = [(there, here) for here, there in shard_moves()]
    own = lax.ppermute(summed, ALL, back).reshape(2, 48, DB)
    low, high = own[0], own[1]
    grad_w_gate = jnp.concatenate([low[:12], low[12:24]], axis=1)
    grad_w_up = jnp.concatenate([high[:12], high[12:24]], axis=1)
    grad_w_input_gate = low[24:36]
    grad_w_down = high[24:]
    grad_norm_gain = summed[0].reshape(48, DB)[36:40].reshape(D)

    grad_factor_two = factor_gradient(sums_two[0], got_two, 1)
    terms_one, got_grad = lax.optimization_barrier((send_each(terms_one, "x"), got_grad))
    sums_one = factor_sums(terms_one)
    got_one = lax.ppermute(sums_one[1], "zh", SWAP)
    grad_factor_one = factor_gradient(sums_one[0], got_one, 4)
    grad_inputs = call(
        join_kernel, (2,), [columns(192, 1024)] * 2, columns(192, 2048), bf(192, 4096), (1, 1)
    )(at, own_grad, got_grad).T
    return (
        mixed_out,
        grad_inputs,
        grad_factor_one,
        grad_factor_two,
        grad_w_input_gate,
        grad_norm_gain,
        grad_w_gate,
        grad_w_up,
        grad_w_down,
    )


def solution(mesh):
    fine = Mesh(mesh.devices.reshape(SIZES), ALL)
    return jax.shard_map(
        per_device,
        mesh=fine,
        in_specs=(
            P(SEQ, CH),
            P(SEQ, None, None),
            P(SEQ, None, None),
            P(ALL, None),
            P(),
            P(ALL, None),
            P(ALL, None),
            P(ALL, None),
            P(ALL, None),
        ),
        out_specs=(
            P(ALL, None),
            P(SEQ, CH),
            P(SEQ, CH, None),
            P(SEQ, CH, None),
            P(ALL, None),
            P(),
            P(ALL, None),
            P(ALL, None),
            P(ALL, None),
        ),
        check_vma=False,
    )
```

```python
import math

import jax
import jax.numpy as jnp
from jax import lax
from jax.experimental import pallas as pl
from jax.experimental.pallas import tpu as pltpu
from jax.sharding import Mesh
from jax.sharding import PartitionSpec as P

D = 1536
NBLK = 4
SEQL = 65536
DB = D // NBLK
BF = jnp.bfloat16
F32 = jnp.float32

SEQ = ("zl", "y", "core")
CH = ("x", "zh")
ALL = SEQ + CH
SIZES = (2, 4, 2, 4, 2)
PLANE = SEQ + ("zh",)


def index_of(zl, y, k, x, zh):
    return (((zl * 4 + y) * 2 + k) * 4 + x) * 2 + zh


def shard_moves():
    moves = []
    for zl in range(2):
        for y in range(4):
            for k in range(2):
                for x in range(4):
                    for zh in range(2):
                        there = index_of(y % 2, k * 2 + x // 2, x % 2, zl * 2 + y // 2, zh)
                        moves.append((index_of(zl, y, k, x, zh), there))
    return moves


SWAP = [(0, 1), (1, 0)]


def call(body, grid, ins, outs, shapes, cost, scratch=()):
    return pl.pallas_call(
        body,
        grid_spec=pltpu.PrefetchScalarGridSpec(
            num_scalar_prefetch=1,
            grid=grid,
            in_specs=ins,
            out_specs=outs,
            scratch_shapes=list(scratch),
        ),
        out_shape=shapes,
        name=body.__name__,
        compiler_params=pltpu.CompilerParams(
            dimension_semantics=("arbitrary",) * len(grid), vmem_limit_bytes=56 * 1024 * 1024
        ),
        cost_estimate=pl.CostEstimate(flops=cost[0], bytes_accessed=cost[1], transcendentals=0),
    )


def whole(*shape):
    return pl.BlockSpec(shape, lambda t, s: (0,) * len(shape))


def rows(width, height=512):
    return pl.BlockSpec((height, width), lambda t, s: (t, 0))


def turned_rows(width, height=512):
    return pl.BlockSpec((height, width), lambda t, s: (lax.rem(s[1] + t, 4), 0))


def columns(height, width=512):
    return pl.BlockSpec((height, width), lambda t, s: (0, t))


PIECES = pl.BlockSpec((32, 2, 8, DB), lambda t, s: (0, t, 0, 0))
SUMS = [whole(8, 512)] * 4


def read_pieces(ref):
    return jnp.concatenate(
        [ref[:, r].astype(F32).reshape(256, DB) for r in range(2)], axis=0
    )


def row_sums(value):
    ones = jnp.ones((8, DB), BF)
    high = value.astype(BF)
    low = (value - high.astype(F32)).astype(BF)
    return dot_t(ones, high) + dot_t(ones, low)


def row_of(refs, at):
    total = refs[0][...] + refs[1][...] + refs[2][...] + refs[3][...]
    here = lax.broadcasted_iota(jnp.int32, (8, 512), 0) == at
    return jnp.sum(jnp.where(here, total, 0.0), axis=0, keepdims=True)


def put_row(ref, at, value):
    here = lax.broadcasted_iota(jnp.int32, (8, 512), 0) == at
    ref[...] = jnp.where(here, value, ref[...])


def as_column(row):
    turned = jnp.transpose(jnp.broadcast_to(row, (128, row.shape[1])))
    return jnp.concatenate([turned] * (DB // 128), axis=1)


def dot(a, b):
    return jnp.dot(a, b, preferred_element_type=F32)


def dot_t(a, b):
    return lax.dot_general(a, b, (((1,), (1,)), ((), ())), preferred_element_type=F32)


def t_dot(a, b):
    return lax.dot_general(a, b, (((0,), (0,)), ((), ())), preferred_element_type=F32)


def sigmoid(value):
    return 0.5 * jnp.tanh(0.5 * value) + 0.5


def first_kernel(_, f1_ref, in_ref, payload_ref, out_ref):
    step = pl.program_id(0)

    @pl.when(step < 8)
    def _():
        results = [
            dot_t(f1_ref[r], in_ref[:, r * 256 : (r + 1) * 256]).reshape(32, 8, 192)
            for r in range(2)
        ]
        out_ref[:, 0] = jnp.concatenate(results, axis=2).astype(BF)

    @pl.when(step >= 8)
    def _():
        halves = [payload_ref[core, lax.max(step - 8, 0)] for core in range(2)]
        for dev in range(32):
            out_ref[dev, 0] = halves[dev // 2 % 2]


def copy_kernel(_, in_ref, out_ref):
    out_ref[...] = in_ref[...]


def copy_three_kernel(_, *refs):
    for j in range(3):
        refs[3 + j][...] = refs[j][...]


def put_rows(refs, row, value):
    for j, ref in enumerate(refs):
        ref[row : row + value.shape[0], :] = value[:, j * 128 : (j + 1) * 128]


def put_position(refs, a, value):
    for j, ref in enumerate(refs):
        ref[pl.ds(a, 256, stride=8), :] = value[:, j * 128 : (j + 1) * 128]


def take_position(refs, a):
    parts = [ref[pl.ds(a, 256, stride=8), :] for ref in refs]
    return jnp.concatenate(parts, axis=1).astype(BF)


def second_kernel(_, piece_ref, f2_ref, out_ref, first_ref, *scratch):
    cols, result = scratch[:3], scratch[3:]
    for s in range(16):
        for pair in range(8):
            low, high = (piece_ref[2 * s + h, pair].astype(F32) for h in range(2))
            row = (s * 16 + pair * 2) * 8
            put_rows(cols, row, jnp.concatenate([low[:, :192], high[:, :192]], axis=1))
            put_rows(cols, row + 8, jnp.concatenate([low[:, 192:], high[:, 192:]], axis=1))
    for a in range(8):
        first = take_position(cols, a)
        first_ref[a] = first
        put_position(result, a, dot(f2_ref[a], first))
    write_blocks(result, out_ref)


def first_grad_kernel(_, piece_ref, f2_ref, keep_ref, got_ref, out_ref, grad_ref, *scratch):
    cols, result = scratch[:3], scratch[3:]
    for dev in range(32):
        s, h = dev // 2, dev % 2
        for x in range(4):
            row = (s * 16 + x * 4 + h * 2) * 8
            put_rows(cols, row, piece_ref[dev, 2 * x : 2 * x + 2].astype(F32).reshape(16, DB))
    for a in range(8):
        grad = take_position(cols, a)
        grad_ref[a] = grad
        put_position(result, a, t_dot(f2_ref[a], grad))
    write_blocks(result, out_ref)
    for dev in range(32):
        total = keep_ref[dev].astype(F32) + got_ref[dev].astype(F32)
        out_ref[dev, 8:] = total.astype(BF)


def write_blocks(result, out_ref):
    for dev in range(32):
        s, h = dev // 2, dev % 2
        for x in range(4):
            row = (s * 16 + x * 4 + h * 2) * 8
            value = jnp.concatenate([ref[row : row + 16, :] for ref in result], axis=1)
            out_ref[dev, 2 * x : 2 * x + 2] = value.reshape(2, 8, DB).astype(BF)


def gating_kernel(s_ref, own_ref, got_ref, second_ref, win_ref, in_ref, resid_ref, pgate_ref, sum_ref):
    zh = s_ref[0]
    own, got = own_ref[...], got_ref[...]
    first_half = jnp.where(zh == 0, own, got)
    second_half = jnp.where(zh == 0, got, own)
    value = jnp.transpose(jnp.concatenate([first_half, second_half], axis=0))
    in_ref[...] = value
    pgate = dot(value, win_ref[...]).astype(BF)
    pgate_ref[...] = pgate
    value_f = value.astype(F32)
    silu_in = value_f * sigmoid(value_f)
    resid = (value_f + read_pieces(second_ref) * pgate.astype(F32) * silu_in).astype(BF)
    resid_ref[...] = resid
    resid_f = resid.astype(F32)

    @pl.when(pl.program_id(0) == 0)
    def _():
        sum_ref[...] = jnp.zeros_like(sum_ref)

    put_row(sum_ref, pl.program_id(0), row_sums(resid_f * resid_f))


def mlp_kernel(s_ref, resid_ref, gain_ref, wg_ref, wu_ref, wd_ref, *refs):
    squares, cots = refs[:4], refs[4:8]
    cot_ref, normed_ref, hidden_ref, grads_ref, gnormed_ref, inner_ref = refs[8:14]
    mixed_refs = refs[14:18]
    step = pl.program_id(0)
    chunk = lax.rem(s_ref[1] + step, 4)
    for j in range(4):

        @pl.when(step == j)
        def _(j=j):
            cot_ref[...] = cots[j][...]

    cot = cot_ref[...]
    resid_f = resid_ref[...].astype(F32)
    rstd = as_column(lax.rsqrt(row_of(squares, chunk) * (1.0 / D) + 1e-06))
    gain = gain_ref[...]
    scaled_resid = resid_f * rstd
    normed = (scaled_resid * gain).astype(BF)
    normed_ref[...] = normed
    gate = dot(normed, wg_ref[...])
    upper = dot(normed, wu_ref[...])
    g_hidden = dot_t(cot, wd_ref[...])
    sig = sigmoid(gate)
    act = gate * sig
    hidden = (act * upper).astype(BF)
    hidden_ref[...] = hidden
    g_gate = (g_hidden * upper * (sig + act * (1.0 - sig))).astype(BF)
    g_up = (g_hidden * act).astype(BF)
    grads_ref[:, :768] = g_gate
    grads_ref[:, 768:] = g_up
    mixed = (resid_f + dot(hidden, wd_ref[...])).astype(BF)
    for j in range(4):

        @pl.when(step == j)
        def _(j=j):
            mixed_refs[j][...] = mixed

    g_normed = dot_t(g_gate, wg_ref[...]) + dot_t(g_up, wu_ref[...])
    gnormed_ref[...] = g_normed

    @pl.when(step == 0)
    def _():
        inner_ref[...] = jnp.zeros_like(inner_ref)

    put_row(inner_ref, chunk, row_sums(g_normed * gain * resid_f))
    inner_ref[4:5, :DB] += jnp.sum(g_normed * scaled_resid, axis=0, keepdims=True)


def resid_grad_kernel(
    _, resid_ref, cot_ref, gain_ref, gnormed_ref, in_ref, pgate_ref, *refs
):
    squares, inners, (g_resid_ref, g_second_ref) = refs[:4], refs[4:8], refs[8:]
    step = pl.program_id(0)
    rstd_row = lax.rsqrt(row_of(squares, step) * (1.0 / D) + 1e-06)
    rstd = as_column(rstd_row)
    factor = as_column(rstd_row * rstd_row * rstd_row * (row_of(inners, step) * (1.0 / D)))
    scaled = gnormed_ref[...] * gain_ref[...]
    g_resid = (
        cot_ref[...].astype(F32) + rstd * scaled - resid_ref[...].astype(F32) * factor
    ).astype(BF)
    g_resid_ref[...] = g_resid
    value = in_ref[...].astype(F32)
    silu_in = value * sigmoid(value)
    g_second = (g_resid.astype(F32) * pgate_ref[...].astype(F32) * silu_in).astype(BF)
    for r in range(2):
        g_second_ref[:, r] = g_second[r * 256 : (r + 1) * 256].reshape(32, 8, DB)


def direct_kernel(_, g_resid_ref, in_ref, second_ref, pgate_ref, win_ref, g_direct_ref, term_ref):
    resid_grad = g_resid_ref[...].astype(F32)
    value = in_ref[...].astype(F32)
    sig = sigmoid(value)
    second = read_pieces(second_ref)
    g_pgate = (resid_grad * second * (value * sig)).astype(BF)
    slope = sig * (1.0 + value * (1.0 - sig))
    through = dot_t(g_pgate, win_ref[...])
    g_direct_ref[...] = jnp.transpose(
        (resid_grad * (1.0 + second * pgate_ref[...].astype(F32) * slope) + through).astype(BF)
    )
    term = t_dot(in_ref[...], g_pgate)

    @pl.when(pl.program_id(0) == 0)
    def _():
        term_ref[...] = jnp.zeros_like(term_ref)

    term_ref[...] += term


def put_terms(s_ref, term, scratch, refs, slot):
    scratch[...] = term * (1.0 / math.sqrt(D))
    for j in range(4):
        start = pl.multiple_of(lax.rem(s_ref[1] + j, 4) * 64, 64)
        refs[j][slot] = scratch[pl.ds(start, 64), :].astype(BF)


def term_two_kernel(s_ref, grad_ref, first_ref, *refs):
    for a in range(2):
        put_terms(s_ref, dot_t(grad_ref[a], first_ref[a]), refs[4], refs[:4], a)


def term_one_kernel(s_ref, g_first_ref, in_ref, *refs):
    for r in range(2):
        g_first = g_first_ref[:, r].reshape(256, DB)
        term = dot_t(g_first, in_ref[r * 256 : (r + 1) * 256])
        put_terms(s_ref, term, refs[4], refs[:4], r)


def factor_sum_kernel(s_ref, a_ref, b_ref, c_ref, d_ref, own_ref, give_ref):
    zh = s_ref[0]
    total = (
        a_ref[...].astype(F32) + b_ref[...].astype(F32)
        + c_ref[...].astype(F32) + d_ref[...].astype(F32)
    )
    low, high = total[:, :32], total[:, 32:]
    own_ref[...] = jnp.where(zh == 0, low, high)
    give_ref[...] = jnp.where(zh == 0, high, low).astype(BF)


def factor_join_kernel(s_ref, own_ref, got_ref, out_ref):
    zh = s_ref[0]
    own, got = own_ref[...], got_ref[...].astype(F32)
    out_ref[:, 0] = jnp.where(zh == 0, own, got)
    out_ref[:, 1] = jnp.where(zh == 0, got, own)


def back_kernel(s_ref, g_first_ref, f1_ref, direct_ref, own_ref, give_ref):
    zh = s_ref[0]
    for r in range(2):
        here = slice(r * 256, (r + 1) * 256)
        back = t_dot(g_first_ref[:, r].reshape(256, DB), f1_ref[0, r])
        total = direct_ref[:, here].astype(F32) + back
        low, high = total[:192], total[192:]
        own_ref[:, here] = jnp.where(zh == 0, low, high).astype(BF)
        give_ref[:, here] = jnp.where(zh == 0, high, low).astype(BF)


def join_kernel(s_ref, own_ref, got_ref, out_ref):
    zh = s_ref[0]
    for q in range(2):
        here = slice(q * 512, (q + 1) * 512)
        own, got = own_ref[:, here], got_ref[:, here]
        out_ref[:, q * 1024 : q * 1024 + 512] = jnp.where(zh == 0, own, got)
        out_ref[:, q * 1024 + 512 : (q + 1) * 1024] = jnp.where(zh == 0, got, own)


def mixed_join_kernel(s_ref, *refs):
    for j in range(4):
        start = pl.multiple_of(lax.rem(s_ref[1] + 4 - j, 4) * DB, DB)
        refs[4][:, pl.ds(start, DB)] = refs[j][...]


def payload_kernel(_, wg_ref, wu_ref, win_ref, wd_ref, out_ref):
    wg, wu = wg_ref[...].astype(F32), wu_ref[...].astype(F32)
    win, down = win_ref[...].astype(F32), wd_ref[...].astype(F32)
    put_half(out_ref, 0, [wg[:, :DB], wg[:, DB:], win, jnp.zeros_like(win)])
    put_half(out_ref, 1, [wu[:, :DB], wu[:, DB:], down])


def put_half(ref, at, parts):
    ref[at] = jnp.concatenate(parts, axis=0).reshape(6, 8, DB).astype(BF)


def gather_kernel(_, *refs):
    for j in range(4):
        refs[4][:, j * 512 : (j + 1) * 512] = refs[j][...]


def weights_kernel(s_ref, own_ref, across_ref, wg_ref, wu_ref, win_ref, wd_ref):
    first = s_ref[4] == 0
    gates, ups, entries, downs = [], [], [], []
    for shard in range(8):
        own = own_ref[shard].astype(F32).reshape(48, DB)
        across = across_ref[shard].astype(F32).reshape(48, DB)
        low, high = jnp.where(first, own, across), jnp.where(first, across, own)
        gates.append(jnp.concatenate([low[:12], low[12:24]], axis=1))
        entries.append(low[24:36])
        ups.append(jnp.concatenate([high[:12], high[12:24]], axis=1))
        downs.append(high[24:])
    for ref, parts in ((wg_ref, gates), (wu_ref, ups), (win_ref, entries), (wd_ref, downs)):
        ref[...] = jnp.concatenate(parts, axis=0).astype(BF)


def weight_grad_kernel(
    s_ref, normed_ref, grads_ref, hidden_ref, cot_ref, entry_ref, *refs,
):
    inners, (keep_ref, give_ref, across, down) = refs[:4], refs[4:]
    step = pl.program_id(0)

    @pl.when(step == 0)
    def _():
        across[...] = jnp.zeros_like(across)
        down[...] = jnp.zeros_like(down)

    across[...] += t_dot(normed_ref[...], grads_ref[...])
    down[...] += t_dot(hidden_ref[...], cot_ref[...])

    @pl.when(step == pl.num_programs(0) - 1)
    def _():
        first = s_ref[4] == 0
        fill = jnp.zeros((8, DB), F32)
        block = lax.broadcasted_iota(jnp.int32, (4, DB), 0)
        gains = jnp.zeros((4, DB), F32)
        for j in range(4):
            mine = jnp.broadcast_to(inners[j][4:5, :DB], (4, DB))
            gains = gains + jnp.where(block == lax.rem(s_ref[1] + j, 4), mine, 0.0)
        for shard in range(32):
            here = slice(shard * 12, shard * 12 + 12)
            gates, entries = across[here, :], entry_ref[here, :]
            low = [gates[:, :DB], gates[:, DB : 2 * DB], entries, gains, fill]
            high = [gates[:, 2 * DB : 3 * DB], gates[:, 3 * DB :]]
            high.append(down[shard * 24 : shard * 24 + 24, :])
            low = jnp.concatenate(low, axis=0)
            high = jnp.concatenate(high, axis=0)
            put_half(keep_ref, shard, [jnp.where(first, low, high)])
            put_half(give_ref, shard, [jnp.where(first, high, low)])


def weight_sum_kernel(_, in_ref, out_ref):
    for core in range(2):
        total = jnp.zeros((2, 8, DB), F32)
        for pair in range(8):
            for zh in range(2):
                total = total + in_ref[pair * 4 + core * 2 + zh].astype(F32)
        out_ref[core] = total * (1.0 / math.sqrt(SEQL))


def turn(axis, size, step):
    return [(i, (i + step) % size) for i in range(size)]


def around(value, axis):
    return [value] + [lax.ppermute(value, axis, turn(axis, 4, -j)) for j in (1, 2, 3)]


def send_each(parts, axis):
    return [parts[0]] + [lax.ppermute(parts[j], axis, turn(axis, 4, j)) for j in (1, 2, 3)]


Z_RING = ("zl", "zh")


def per_device(
    inputs, factor_one, factor_two, w_input_gate, norm_gain, w_gate, w_up, w_down, grad_out
):
    tok_scale = 1.0 / math.sqrt(SEQL)
    zh = lax.axis_index("zh")
    xi = lax.axis_index("x")
    yi = lax.axis_index("y")
    core = lax.axis_index("core")
    zi = lax.axis_index("zl") * 2 + zh
    at = jnp.stack([zh, xi, yi, zi, core]).astype(jnp.int32)
    bf = lambda *shape: jax.ShapeDtypeStruct(shape, BF)
    f32 = lambda *shape: jax.ShapeDtypeStruct(shape, F32)
    turned_in = inputs.T

    give = call(
        gather_kernel, (1,),
        [pl.BlockSpec((192, 512), lambda t, s, q=q: (0, 2 * q + 1 - s[0])) for q in range(4)],
        whole(192, 2048), bf(192, 2048), (1, 1),
    )(at, *[turned_in] * 4)
    other = lax.ppermute(give, "zh", SWAP)
    give, turned_in, w_gate = lax.optimization_barrier((give, turned_in, w_gate))

    payload = call(
        payload_kernel, (1,),
        [whole(12, 768), whole(12, 768), whole(12, DB), whole(24, DB)],
        whole(2, 6, 8, DB), bf(2, 6, 8, DB), (1, 1),
    )(at, w_gate, w_up, w_input_gate, w_down)
    payload = lax.ppermute(payload, ALL, shard_moves())
    first_local = call(
        first_kernel, (14,),
        [pl.BlockSpec((2, 256, 256), lambda t, s: (lax.min(t, 7), 0, 0)),
         pl.BlockSpec((192, 512), lambda t, s: (0, lax.min(t, 7))), whole(2, 6, 8, DB)],
        pl.BlockSpec((32, 1, 8, DB), lambda t, s: (0, t, 0, 0)),
        bf(32, 14, 8, DB),
        (1, 1),
    )(at, factor_one, turned_in, payload)
    first_local, other, turned_in, grad_out, factor_two = lax.optimization_barrier(
        (first_local, other, turned_in, grad_out, factor_two)
    )
    piece = lax.all_to_all(first_local, PLANE, split_axis=0, concat_axis=0, tiled=True)
    gain = lax.dynamic_slice_in_dim(norm_gain, xi * DB, DB, 0).reshape(1, DB)

    to_send = call(
        copy_three_kernel, (1,),
        [pl.BlockSpec((512, DB), lambda t, s, j=j: (0, lax.rem(s[1] + 4 - j, 4))) for j in (1, 2, 3)],
        [whole(512, DB)] * 3, [bf(512, DB)] * 3, (1, 1),
    )(at, grad_out, grad_out, grad_out)
    cots = [lax.ppermute(to_send[j - 1], "x", turn("x", 4, -j)) for j in (1, 2, 3)]
    f2 = lax.dynamic_slice_in_dim(factor_two, zh * 8, 8, 0)

    wide = [pltpu.VMEM((2048, 128), F32)] * 6
    all_pieces = whole(32, 8, 8, DB)
    second_cols, first_cols = call(
        second_kernel, (1,),
        [whole(32, 14, 8, DB), whole(8, 256, 256)],
        [all_pieces, whole(8, 256, DB)],
        [bf(32, 8, 8, DB), bf(8, 256, DB)],
        (400_000_000, 6_000_000), wide,
    )(at, piece, f2)
    second_cols, piece = lax.optimization_barrier((second_cols, piece))
    second = lax.all_to_all(second_cols, PLANE, split_axis=0, concat_axis=0, tiled=True)

    half = piece[:, 8:]
    across = lax.ppermute(half, "core", SWAP)
    shards = pl.BlockSpec((8, 6, 8, DB), lambda t, s: (t, 0, 0, 0))
    wg, wu, win, wd = call(
        weights_kernel, (4,), [shards] * 2,
        [rows(768, 96), rows(768, 96), rows(DB, 96), rows(DB, 192)],
        [bf(DB, 768), bf(DB, 768), bf(DB, DB), bf(768, DB)], (1, 1),
    )(at, half, across)

    input_mlp, resid, pgate, square = call(
        gating_kernel, (4,),
        [pl.BlockSpec((192, 512), lambda t, s: (0, 2 * t + s[0])),
         columns(192), PIECES, whole(DB, DB)],
        [rows(DB), rows(DB), rows(DB), whole(8, 512)],
        [bf(2048, DB), bf(2048, DB), bf(2048, DB), f32(8, 512)],
        (600_000_000, 10_000_000),
    )(at, turned_in, other, second, win)
    squares = around(square, "x")
    own_cot = pl.BlockSpec((512, DB), lambda t, s: (0, s[1]))
    cot, normed, hidden, grads, g_normed, inner, *mixed = call(
        mlp_kernel, (4,),
        [turned_rows(DB), whole(1, DB), whole(DB, 768), whole(DB, 768), whole(768, DB)]
        + SUMS + [own_cot] + [whole(512, DB)] * 3,
        [turned_rows(DB), turned_rows(DB), turned_rows(768), turned_rows(1536), turned_rows(DB), whole(8, 512)]
        + [whole(512, DB)] * 4,
        [bf(2048, DB), bf(2048, DB), bf(2048, 768), bf(2048, 1536), f32(2048, DB), f32(8, 512)]
        + [bf(512, DB)] * 4,
        (7_300_000_000, 24_000_000),
    )(at, resid, gain, wg, wu, wd, *squares, grad_out, *cots)
    inners = around(inner, "x")
    g_resid, g_second = call(
        resid_grad_kernel, (4,),
        [rows(DB), rows(DB), whole(1, DB), rows(DB), rows(DB), rows(DB)] + SUMS + SUMS,
        [rows(DB), PIECES],
        [bf(2048, DB), bf(32, 8, 8, DB)],
        (50_000_000, 12_000_000),
    )(at, resid, cot, gain, g_normed, input_mlp, pgate, *squares, *inners)
    g_second, normed, hidden, grads, cot, mixed, inners = lax.optimization_barrier(
        (g_second, normed, hidden, grads, cot, mixed, inners)
    )
    piece = lax.all_to_all(g_second, PLANE, split_axis=0, concat_axis=0, tiled=True)

    mixed = send_each(mixed, "x")
    mixed_out = call(
        mixed_join_kernel, (1,), [whole(512, DB)] * 4, whole(512, D),
        bf(512, D), (1, 1),
    )(at, *mixed)
    g_direct, term_entry = call(
        direct_kernel, (4,),
        [rows(DB), rows(DB), PIECES, rows(DB), whole(DB, DB)],
        [columns(DB), whole(DB, DB)],
        [bf(DB, 2048), f32(DB, DB)],
        (1, 1),
    )(at, g_resid, input_mlp, second, pgate, win)

    halves = whole(32, 6, 8, DB)
    keep, give = call(
        weight_grad_kernel, (2,),
        [rows(DB, 1024), rows(1536, 1024), rows(768, 1024), rows(DB, 1024), whole(DB, DB)] + SUMS,
        [halves] * 2, [bf(32, 6, 8, DB)] * 2, (1, 1),
        [pltpu.VMEM((DB, 1536), F32), pltpu.VMEM((768, DB), F32)],
    )(at, normed, grads, hidden, cot, term_entry, *inners)
    got = lax.ppermute(give, "core", SWAP)

    first_grad, second_grad = call(
        first_grad_kernel, (1,),
        [all_pieces, whole(8, 256, 256), halves, halves],
        [whole(32, 14, 8, DB), whole(8, 256, DB)],
        [bf(32, 14, 8, DB), bf(8, 256, DB)],
        (400_000_000, 6_000_000), wide,
    )(at, piece, f2, keep, got)
    square_scratch = [pltpu.VMEM((256, 256), F32)]
    term_out = pl.BlockSpec((2, 64, 256), lambda t, s: (t, 0, 0))

    first_grad, second_grad = lax.optimization_barrier((first_grad, second_grad))
    g_first = lax.all_to_all(first_grad, PLANE, split_axis=0, concat_axis=0, tiled=True)

    def factor_sums(terms):
        return call(
            factor_sum_kernel, (1,), [whole(8, 64, 256)] * 4, [whole(8, 32, 256)] * 2,
            [f32(8, 32, 256), bf(8, 32, 256)], (1, 1),
        )(at, *terms)

    def factor_gradient(own, got, slots):
        shape = (slots, 8 // slots, 32, 256)
        joined = call(
            factor_join_kernel, (1,), [whole(*shape)] * 2, whole(slots, 2, 8 // slots, 32, 256),
            f32(slots, 2, 8 // slots, 32, 256), (1, 1),
        )(at, own.reshape(shape), got.reshape(shape))
        return joined.reshape(16, 32, 256)

    terms_two = call(
        term_two_kernel, (4,),
        [pl.BlockSpec((2, 256, DB), lambda t, s: (t, 0, 0))] * 2,
        [term_out] * 4, [bf(8, 64, 256)] * 4, (1, 1), square_scratch,
    )(at, second_grad, first_cols)
    sums_two = factor_sums(send_each(terms_two, "x"))

    g_first, sums_two, mixed_out = lax.optimization_barrier((g_first, sums_two, mixed_out))
    own_grad, give_grad = call(
        back_kernel, (4,),
        [PIECES, pl.BlockSpec((1, 2, 256, 256), lambda t, s: (2 * t + s[0], 0, 0, 0)), columns(DB)],
        [columns(192), columns(192)],
        [bf(192, 2048), bf(192, 2048)],
        (12_000_000_000, 6_000_000),
    )(at, g_first, factor_one.reshape(8, 2, 256, 256), g_direct)
    got_two = lax.ppermute(sums_two[1], "zh", SWAP)
    g_first, give_grad, got_two = lax.optimization_barrier((g_first, give_grad, got_two))
    terms_one = call(
        term_one_kernel, (4,), [PIECES, rows(DB)],
        [term_out] * 4, [bf(8, 64, 256)] * 4, (1, 1), square_scratch,
    )(at, g_first, input_mlp)

    got_two, terms_one = lax.optimization_barrier((got_two, terms_one))
    terms_one = send_each(terms_one, "x")
    for_sums, terms_one = lax.optimization_barrier((g_first, terms_one))
    got_grad = lax.ppermute(give_grad, "zh", SWAP)
    summed = call(
        weight_sum_kernel, (3,),
        [pl.BlockSpec((32, 2, 8, DB), lambda t, s: (0, t + 4, 0, 0))],
        pl.BlockSpec((2, 2, 8, DB), lambda t, s: (0, t, 0, 0)), f32(2, 6, 8, DB), (1, 1),
    )(at, for_sums)
    back = [(there, here) for here, there in shard_moves()]
    own = lax.ppermute(summed, ALL, back).reshape(2, 48, DB)
    low, high = own[0], own[1]
    grad_w_gate = jnp.concatenate([low[:12], low[12:24]], axis=1)
    grad_w_up = jnp.concatenate([high[:12], high[12:24]], axis=1)
    grad_w_input_gate = low[24:36]
    grad_w_down = high[24:]
    grad_norm_gain = summed[0].reshape(48, DB)[36:40].reshape(D)

    grad_factor_two = factor_gradient(sums_two[0], got_two, 1)
    sums_one = factor_sums(terms_one)
    got_one = lax.ppermute(sums_one[1], "zh", SWAP)
    grad_factor_one = factor_gradient(sums_one[0], got_one, 4)
    grad_inputs = call(
        join_kernel, (2,), [columns(192, 1024)] * 2, columns(192, 2048), bf(192, 4096), (1, 1)
    )(at, own_grad, got_grad).T
    return (
        mixed_out,
        grad_inputs,
        grad_factor_one,
        grad_factor_two,
        grad_w_input_gate,
        grad_norm_gain,
        grad_w_gate,
        grad_w_up,
        grad_w_down,
    )


def solution(mesh):
    fine = Mesh(mesh.devices.reshape(SIZES), ALL)
    return jax.shard_map(
        per_device,
        mesh=fine,
        in_specs=(
            P(SEQ, CH),
            P(SEQ, None, None),
            P(SEQ, None, None),
            P(ALL, None),
            P(),
            P(ALL, None),
            P(ALL, None),
            P(ALL, None),
            P(ALL, None),
        ),
        out_specs=(
            P(ALL, None),
            P(SEQ, CH),
            P(SEQ, CH, None),
            P(SEQ, CH, None),
            P(ALL, None),
            P(),
            P(ALL, None),
            P(ALL, None),
            P(ALL, None),
        ),
        check_vma=False,
    )
```

```python
import math

import jax
import jax.numpy as jnp
from jax import lax
from jax.experimental import pallas as pl
from jax.experimental.pallas import tpu as pltpu
from jax.sharding import Mesh
from jax.sharding import PartitionSpec as P

D = 1536
NBLK = 4
SEQL = 65536
DB = D // NBLK
BF = jnp.bfloat16
F32 = jnp.float32

SEQ = ("zl", "y", "core")
CH = ("x", "zh")
ALL = SEQ + CH
SIZES = (2, 4, 2, 4, 2)
PLANE = SEQ + ("zh",)


def index_of(zl, y, k, x, zh):
    return (((zl * 4 + y) * 2 + k) * 4 + x) * 2 + zh


def shard_moves():
    moves = []
    for zl in range(2):
        for y in range(4):
            for k in range(2):
                for x in range(4):
                    for zh in range(2):
                        there = index_of(y % 2, k * 2 + x // 2, x % 2, zl * 2 + y // 2, zh)
                        moves.append((index_of(zl, y, k, x, zh), there))
    return moves


SWAP = [(0, 1), (1, 0)]


def call(body, grid, ins, outs, shapes, cost, scratch=()):
    return pl.pallas_call(
        body,
        grid_spec=pltpu.PrefetchScalarGridSpec(
            num_scalar_prefetch=1,
            grid=grid,
            in_specs=ins,
            out_specs=outs,
            scratch_shapes=list(scratch),
        ),
        out_shape=shapes,
        name=body.__name__,
        compiler_params=pltpu.CompilerParams(
            dimension_semantics=("arbitrary",) * len(grid), vmem_limit_bytes=56 * 1024 * 1024
        ),
        cost_estimate=pl.CostEstimate(flops=cost[0], bytes_accessed=cost[1], transcendentals=0),
    )


def whole(*shape):
    return pl.BlockSpec(shape, lambda t, s: (0,) * len(shape))


def rows(width, height=512):
    return pl.BlockSpec((height, width), lambda t, s: (t, 0))


def turned_rows(width, height=512):
    return pl.BlockSpec((height, width), lambda t, s: (lax.rem(s[1] + t, 4), 0))


def columns(height, width=512):
    return pl.BlockSpec((height, width), lambda t, s: (0, t))


PIECES = pl.BlockSpec((32, 2, 8, DB), lambda t, s: (0, t, 0, 0))
SUMS = [whole(8, 512)] * 4


def read_pieces(ref):
    return jnp.concatenate(
        [ref[:, r].astype(F32).reshape(256, DB) for r in range(2)], axis=0
    )


def row_sums(value):
    ones = jnp.ones((8, DB), BF)
    high = value.astype(BF)
    low = (value - high.astype(F32)).astype(BF)
    return dot_t(ones, high) + dot_t(ones, low)


def row_of(refs, at):
    total = refs[0][...] + refs[1][...] + refs[2][...] + refs[3][...]
    here = lax.broadcasted_iota(jnp.int32, (8, 512), 0) == at
    return jnp.sum(jnp.where(here, total, 0.0), axis=0, keepdims=True)


def put_row(ref, at, value):
    here = lax.broadcasted_iota(jnp.int32, (8, 512), 0) == at
    ref[...] = jnp.where(here, value, ref[...])


def as_column(row):
    turned = jnp.transpose(jnp.broadcast_to(row, (128, row.shape[1])))
    return jnp.concatenate([turned] * (DB // 128), axis=1)


def dot(a, b):
    return jnp.dot(a, b, preferred_element_type=F32)


def dot_t(a, b):
    return lax.dot_general(a, b, (((1,), (1,)), ((), ())), preferred_element_type=F32)


def t_dot(a, b):
    return lax.dot_general(a, b, (((0,), (0,)), ((), ())), preferred_element_type=F32)


def sigmoid(value):
    return 0.5 * jnp.tanh(0.5 * value) + 0.5


def first_kernel(_, f1_ref, in_ref, payload_ref, out_ref):
    step = pl.program_id(0)

    @pl.when(step < 4)
    def _():
        for q in range(2):
            results = []
            for r in range(2 * q, 2 * q + 2):
                value = dot_t(f1_ref[r], in_ref[:, r * 256 : (r + 1) * 256])
                results.append(value.reshape(32, 8, 192))
            out_ref[:, q] = jnp.concatenate(results, axis=2).astype(BF)

    @pl.when(step >= 4)
    def _():
        for q in range(2):
            slot = lax.max(2 * step - 8, 0) + q
            halves = [payload_ref[core, slot] for core in range(2)]
            for dev in range(32):
                out_ref[dev, q] = halves[dev // 2 % 2]


def copy_kernel(_, in_ref, out_ref):
    out_ref[...] = in_ref[...]


def copy_three_kernel(_, *refs):
    for j in range(3):
        refs[3 + j][...] = refs[j][...]


def put_rows(refs, row, value):
    for j, ref in enumerate(refs):
        ref[row : row + value.shape[0], :] = value[:, j * 128 : (j + 1) * 128]


def put_position(refs, a, value):
    for j, ref in enumerate(refs):
        ref[pl.ds(a, 256, stride=8), :] = value[:, j * 128 : (j + 1) * 128]


def take_position(refs, a):
    parts = [ref[pl.ds(a, 256, stride=8), :] for ref in refs]
    return jnp.concatenate(parts, axis=1).astype(BF)


def second_kernel(_, piece_ref, f2_ref, out_ref, first_ref, *scratch):
    cols, result = scratch[:3], scratch[3:]
    for s in range(16):
        for pair in range(8):
            low, high = (piece_ref[2 * s + h, pair].astype(F32) for h in range(2))
            row = (s * 16 + pair * 2) * 8
            put_rows(cols, row, jnp.concatenate([low[:, :192], high[:, :192]], axis=1))
            put_rows(cols, row + 8, jnp.concatenate([low[:, 192:], high[:, 192:]], axis=1))
    for a in range(8):
        first = take_position(cols, a)
        first_ref[a] = first
        put_position(result, a, dot(f2_ref[a], first))
    write_blocks(result, out_ref)


def first_grad_kernel(_, piece_ref, f2_ref, keep_ref, got_ref, out_ref, grad_ref, *scratch):
    cols, result = scratch[:3], scratch[3:]
    for dev in range(32):
        s, h = dev // 2, dev % 2
        for x in range(4):
            row = (s * 16 + x * 4 + h * 2) * 8
            put_rows(cols, row, piece_ref[dev, 2 * x : 2 * x + 2].astype(F32).reshape(16, DB))
    for a in range(8):
        grad = take_position(cols, a)
        grad_ref[a] = grad
        put_position(result, a, t_dot(f2_ref[a], grad))
    write_blocks(result, out_ref)
    for dev in range(32):
        total = keep_ref[dev].astype(F32) + got_ref[dev].astype(F32)
        out_ref[dev, 8:] = total.astype(BF)


def write_blocks(result, out_ref):
    for dev in range(32):
        s, h = dev // 2, dev % 2
        for x in range(4):
            row = (s * 16 + x * 4 + h * 2) * 8
            value = jnp.concatenate([ref[row : row + 16, :] for ref in result], axis=1)
            out_ref[dev, 2 * x : 2 * x + 2] = value.reshape(2, 8, DB).astype(BF)


def gating_kernel(s_ref, own_ref, got_ref, second_ref, win_ref, in_ref, resid_ref, pgate_ref, sum_ref):
    zh = s_ref[0]
    own, got = own_ref[...], got_ref[...]
    first_half = jnp.where(zh == 0, own, got)
    second_half = jnp.where(zh == 0, got, own)
    value = jnp.transpose(jnp.concatenate([first_half, second_half], axis=0))
    in_ref[...] = value
    pgate = dot(value, win_ref[...]).astype(BF)
    pgate_ref[...] = pgate
    value_f = value.astype(F32)
    silu_in = value_f * sigmoid(value_f)
    resid = (value_f + read_pieces(second_ref) * pgate.astype(F32) * silu_in).astype(BF)
    resid_ref[...] = resid
    resid_f = resid.astype(F32)

    @pl.when(pl.program_id(0) == 0)
    def _():
        sum_ref[...] = jnp.zeros_like(sum_ref)

    put_row(sum_ref, pl.program_id(0), row_sums(resid_f * resid_f))


def mlp_kernel(s_ref, resid_ref, gain_ref, wg_ref, wu_ref, wd_ref, *refs):
    squares, cots = refs[:4], refs[4:8]
    cot_ref, normed_ref, hidden_ref, grads_ref, gnormed_ref, inner_ref = refs[8:14]
    mixed_refs = refs[14:18]
    step = pl.program_id(0)
    chunk = lax.rem(s_ref[1] + step, 4)
    for j in range(4):

        @pl.when(step == j)
        def _(j=j):
            cot_ref[...] = cots[j][...]

    cot = cot_ref[...]
    resid_f = resid_ref[...].astype(F32)
    rstd = as_column(lax.rsqrt(row_of(squares, chunk) * (1.0 / D) + 1e-06))
    gain = gain_ref[...]
    scaled_resid = resid_f * rstd
    normed = (scaled_resid * gain).astype(BF)
    normed_ref[...] = normed
    gate = dot(normed, wg_ref[...])
    upper = dot(normed, wu_ref[...])
    g_hidden = dot_t(cot, wd_ref[...])
    sig = sigmoid(gate)
    act = gate * sig
    hidden = (act * upper).astype(BF)
    hidden_ref[...] = hidden
    g_gate = (g_hidden * upper * (sig + act * (1.0 - sig))).astype(BF)
    g_up = (g_hidden * act).astype(BF)
    grads_ref[:, :768] = g_gate
    grads_ref[:, 768:] = g_up
    mixed = (resid_f + dot(hidden, wd_ref[...])).astype(BF)
    for j in range(4):

        @pl.when(step == j)
        def _(j=j):
            mixed_refs[j][...] = mixed

    g_normed = dot_t(g_gate, wg_ref[...]) + dot_t(g_up, wu_ref[...])
    gnormed_ref[...] = g_normed

    @pl.when(step == 0)
    def _():
        inner_ref[...] = jnp.zeros_like(inner_ref)

    put_row(inner_ref, chunk, row_sums(g_normed * gain * resid_f))
    inner_ref[4:5, :DB] += jnp.sum(g_normed * scaled_resid, axis=0, keepdims=True)


def resid_grad_kernel(
    _, resid_ref, cot_ref, gain_ref, gnormed_ref, in_ref, pgate_ref, *refs
):
    squares, inners, (g_resid_ref, g_second_ref) = refs[:4], refs[4:8], refs[8:]
    step = pl.program_id(0)
    rstd_row = lax.rsqrt(row_of(squares, step) * (1.0 / D) + 1e-06)
    rstd = as_column(rstd_row)
    factor = as_column(rstd_row * rstd_row * rstd_row * (row_of(inners, step) * (1.0 / D)))
    scaled = gnormed_ref[...] * gain_ref[...]
    g_resid = (
        cot_ref[...].astype(F32) + rstd * scaled - resid_ref[...].astype(F32) * factor
    ).astype(BF)
    g_resid_ref[...] = g_resid
    value = in_ref[...].astype(F32)
    silu_in = value * sigmoid(value)
    g_second = (g_resid.astype(F32) * pgate_ref[...].astype(F32) * silu_in).astype(BF)
    for r in range(2):
        g_second_ref[:, r] = g_second[r * 256 : (r + 1) * 256].reshape(32, 8, DB)


def direct_kernel(_, g_resid_ref, in_ref, second_ref, pgate_ref, win_ref, g_direct_ref, term_ref):
    resid_grad = g_resid_ref[...].astype(F32)
    value = in_ref[...].astype(F32)
    sig = sigmoid(value)
    second = read_pieces(second_ref)
    g_pgate = (resid_grad * second * (value * sig)).astype(BF)
    slope = sig * (1.0 + value * (1.0 - sig))
    through = dot_t(g_pgate, win_ref[...])
    g_direct_ref[...] = jnp.transpose(
        (resid_grad * (1.0 + second * pgate_ref[...].astype(F32) * slope) + through).astype(BF)
    )
    term = t_dot(in_ref[...], g_pgate)

    @pl.when(pl.program_id(0) == 0)
    def _():
        term_ref[...] = jnp.zeros_like(term_ref)

    term_ref[...] += term


def put_terms(s_ref, term, scratch, refs, slot):
    scratch[...] = term * (1.0 / math.sqrt(D))
    for j in range(4):
        start = pl.multiple_of(lax.rem(s_ref[1] + j, 4) * 64, 64)
        refs[j][slot] = scratch[pl.ds(start, 64), :].astype(BF)


def term_two_kernel(s_ref, grad_ref, first_ref, *refs):
    for a in range(2):
        put_terms(s_ref, dot_t(grad_ref[a], first_ref[a]), refs[4], refs[:4], a)


def term_one_kernel(s_ref, g_first_ref, in_ref, *refs):
    for r in range(2):
        g_first = g_first_ref[:, r].reshape(256, DB)
        term = dot_t(g_first, in_ref[r * 256 : (r + 1) * 256])
        put_terms(s_ref, term, refs[4], refs[:4], r)


def factor_sum_kernel(s_ref, a_ref, b_ref, c_ref, d_ref, own_ref, give_ref):
    zh = s_ref[0]
    total = (
        a_ref[...].astype(F32) + b_ref[...].astype(F32)
        + c_ref[...].astype(F32) + d_ref[...].astype(F32)
    )
    low, high = total[:, :32], total[:, 32:]
    own_ref[...] = jnp.where(zh == 0, low, high)
    give_ref[...] = jnp.where(zh == 0, high, low).astype(BF)


def factor_join_kernel(s_ref, own_ref, got_ref, out_ref):
    zh = s_ref[0]
    own, got = own_ref[...], got_ref[...].astype(F32)
    out_ref[:, 0] = jnp.where(zh == 0, own, got)
    out_ref[:, 1] = jnp.where(zh == 0, got, own)


def back_kernel(s_ref, g_first_ref, f1_ref, direct_ref, own_ref, give_ref):
    zh = s_ref[0]
    for r in range(2):
        here = slice(r * 256, (r + 1) * 256)
        back = t_dot(g_first_ref[:, r].reshape(256, DB), f1_ref[0, r])
        total = direct_ref[:, here].astype(F32) + back
        low, high = total[:192], total[192:]
        own_ref[:, here] = jnp.where(zh == 0, low, high).astype(BF)
        give_ref[:, here] = jnp.where(zh == 0, high, low).astype(BF)


def join_kernel(s_ref, own_ref, got_ref, out_ref):
    zh = s_ref[0]
    for q in range(2):
        here = slice(q * 512, (q + 1) * 512)
        own, got = own_ref[:, here], got_ref[:, here]
        out_ref[:, q * 1024 : q * 1024 + 512] = jnp.where(zh == 0, own, got)
        out_ref[:, q * 1024 + 512 : (q + 1) * 1024] = jnp.where(zh == 0, got, own)


def mixed_join_kernel(s_ref, *refs):
    for j in range(4):
        start = pl.multiple_of(lax.rem(s_ref[1] + 4 - j, 4) * DB, DB)
        refs[4][:, pl.ds(start, DB)] = refs[j][...]


def payload_kernel(_, wg_ref, wu_ref, win_ref, wd_ref, out_ref):
    wg, wu = wg_ref[...].astype(F32), wu_ref[...].astype(F32)
    win, down = win_ref[...].astype(F32), wd_ref[...].astype(F32)
    put_half(out_ref, 0, [wg[:, :DB], wg[:, DB:], win, jnp.zeros_like(win)])
    put_half(out_ref, 1, [wu[:, :DB], wu[:, DB:], down])


def put_half(ref, at, parts):
    ref[at] = jnp.concatenate(parts, axis=0).reshape(6, 8, DB).astype(BF)


def gather_kernel(_, *refs):
    for j in range(4):
        refs[4][:, j * 512 : (j + 1) * 512] = refs[j][...]


def weights_kernel(s_ref, own_ref, across_ref, wg_ref, wu_ref, win_ref, wd_ref):
    first = s_ref[4] == 0
    gates, ups, entries, downs = [], [], [], []
    for shard in range(8):
        own = own_ref[shard].astype(F32).reshape(48, DB)
        across = across_ref[shard].astype(F32).reshape(48, DB)
        low, high = jnp.where(first, own, across), jnp.where(first, across, own)
        gates.append(jnp.concatenate([low[:12], low[12:24]], axis=1))
        entries.append(low[24:36])
        ups.append(jnp.concatenate([high[:12], high[12:24]], axis=1))
        downs.append(high[24:])
    for ref, parts in ((wg_ref, gates), (wu_ref, ups), (win_ref, entries), (wd_ref, downs)):
        ref[...] = jnp.concatenate(parts, axis=0).astype(BF)


def weight_grad_kernel(
    s_ref, normed_ref, grads_ref, hidden_ref, cot_ref, entry_ref, *refs,
):
    inners, (keep_ref, give_ref, across, down) = refs[:4], refs[4:]
    step = pl.program_id(0)

    @pl.when(step == 0)
    def _():
        across[...] = jnp.zeros_like(across)
        down[...] = jnp.zeros_like(down)

    across[...] += t_dot(normed_ref[...], grads_ref[...])
    down[...] += t_dot(hidden_ref[...], cot_ref[...])

    @pl.when(step == pl.num_programs(0) - 1)
    def _():
        first = s_ref[4] == 0
        fill = jnp.zeros((8, DB), F32)
        block = lax.broadcasted_iota(jnp.int32, (4, DB), 0)
        gains = jnp.zeros((4, DB), F32)
        for j in range(4):
            mine = jnp.broadcast_to(inners[j][4:5, :DB], (4, DB))
            gains = gains + jnp.where(block == lax.rem(s_ref[1] + j, 4), mine, 0.0)
        for shard in range(32):
            here = slice(shard * 12, shard * 12 + 12)
            gates, entries = across[here, :], entry_ref[here, :]
            low = [gates[:, :DB], gates[:, DB : 2 * DB], entries, gains, fill]
            high = [gates[:, 2 * DB : 3 * DB], gates[:, 3 * DB :]]
            high.append(down[shard * 24 : shard * 24 + 24, :])
            low = jnp.concatenate(low, axis=0)
            high = jnp.concatenate(high, axis=0)
            put_half(keep_ref, shard, [jnp.where(first, low, high)])
            put_half(give_ref, shard, [jnp.where(first, high, low)])


def weight_sum_kernel(_, in_ref, out_ref):
    for core in range(2):
        total = jnp.zeros((2, 8, DB), F32)
        for pair in range(8):
            for zh in range(2):
                total = total + in_ref[pair * 4 + core * 2 + zh].astype(F32)
        out_ref[core] = total * (1.0 / math.sqrt(SEQL))


def turn(axis, size, step):
    return [(i, (i + step) % size) for i in range(size)]


def around(value, axis):
    return [value] + [lax.ppermute(value, axis, turn(axis, 4, -j)) for j in (1, 2, 3)]


def send_each(parts, axis):
    return [parts[0]] + [lax.ppermute(parts[j], axis, turn(axis, 4, j)) for j in (1, 2, 3)]


Z_RING = ("zl", "zh")


def per_device(
    inputs, factor_one, factor_two, w_input_gate, norm_gain, w_gate, w_up, w_down, grad_out
):
    tok_scale = 1.0 / math.sqrt(SEQL)
    zh = lax.axis_index("zh")
    xi = lax.axis_index("x")
    yi = lax.axis_index("y")
    core = lax.axis_index("core")
    zi = lax.axis_index("zl") * 2 + zh
    at = jnp.stack([zh, xi, yi, zi, core]).astype(jnp.int32)
    bf = lambda *shape: jax.ShapeDtypeStruct(shape, BF)
    f32 = lambda *shape: jax.ShapeDtypeStruct(shape, F32)
    turned_in = inputs.T

    give = call(
        gather_kernel, (1,),
        [pl.BlockSpec((192, 512), lambda t, s, q=q: (0, 2 * q + 1 - s[0])) for q in range(4)],
        whole(192, 2048), bf(192, 2048), (1, 1),
    )(at, *[turned_in] * 4)
    other = lax.ppermute(give, "zh", SWAP)
    give, turned_in, w_gate = lax.optimization_barrier((give, turned_in, w_gate))

    payload = call(
        payload_kernel, (1,),
        [whole(12, 768), whole(12, 768), whole(12, DB), whole(24, DB)],
        whole(2, 6, 8, DB), bf(2, 6, 8, DB), (1, 1),
    )(at, w_gate, w_up, w_input_gate, w_down)
    payload = lax.ppermute(payload, ALL, shard_moves())
    first_local = call(
        first_kernel, (7,),
        [pl.BlockSpec((4, 256, 256), lambda t, s: (lax.min(t, 3), 0, 0)),
         pl.BlockSpec((192, 1024), lambda t, s: (0, lax.min(t, 3))), whole(2, 6, 8, DB)],
        pl.BlockSpec((32, 2, 8, DB), lambda t, s: (0, t, 0, 0)),
        bf(32, 14, 8, DB),
        (1, 1),
    )(at, factor_one, turned_in, payload)
    first_local, other, turned_in, grad_out, factor_two = lax.optimization_barrier(
        (first_local, other, turned_in, grad_out, factor_two)
    )
    piece = lax.all_to_all(first_local, PLANE, split_axis=0, concat_axis=0, tiled=True)
    gain = lax.dynamic_slice_in_dim(norm_gain, xi * DB, DB, 0).reshape(1, DB)

    to_send = call(
        copy_three_kernel, (1,),
        [pl.BlockSpec((512, DB), lambda t, s, j=j: (0, lax.rem(s[1] + 4 - j, 4))) for j in (1, 2, 3)],
        [whole(512, DB)] * 3, [bf(512, DB)] * 3, (1, 1),
    )(at, grad_out, grad_out, grad_out)
    cots = [lax.ppermute(to_send[j - 1], "x", turn("x", 4, -j)) for j in (1, 2, 3)]
    f2 = lax.dynamic_slice_in_dim(factor_two, zh * 8, 8, 0)

    wide = [pltpu.VMEM((2048, 128), F32)] * 6
    all_pieces = whole(32, 8, 8, DB)
    second_cols, first_cols = call(
        second_kernel, (1,),
        [whole(32, 14, 8, DB), whole(8, 256, 256)],
        [all_pieces, whole(8, 256, DB)],
        [bf(32, 8, 8, DB), bf(8, 256, DB)],
        (400_000_000, 6_000_000), wide,
    )(at, piece, f2)
    second_cols, piece = lax.optimization_barrier((second_cols, piece))
    second = lax.all_to_all(second_cols, PLANE, split_axis=0, concat_axis=0, tiled=True)

    half = piece[:, 8:]
    across = lax.ppermute(half, "core", SWAP)
    shards = pl.BlockSpec((8, 6, 8, DB), lambda t, s: (t, 0, 0, 0))
    wg, wu, win, wd = call(
        weights_kernel, (4,), [shards] * 2,
        [rows(768, 96), rows(768, 96), rows(DB, 96), rows(DB, 192)],
        [bf(DB, 768), bf(DB, 768), bf(DB, DB), bf(768, DB)], (1, 1),
    )(at, half, across)

    input_mlp, resid, pgate, square = call(
        gating_kernel, (4,),
        [pl.BlockSpec((192, 512), lambda t, s: (0, 2 * t + s[0])),
         columns(192), PIECES, whole(DB, DB)],
        [rows(DB), rows(DB), rows(DB), whole(8, 512)],
        [bf(2048, DB), bf(2048, DB), bf(2048, DB), f32(8, 512)],
        (600_000_000, 10_000_000),
    )(at, turned_in, other, second, win)
    squares = around(square, "x")
    own_cot = pl.BlockSpec((512, DB), lambda t, s: (0, s[1]))
    cot, normed, hidden, grads, g_normed, inner, *mixed = call(
        mlp_kernel, (4,),
        [turned_rows(DB), whole(1, DB), whole(DB, 768), whole(DB, 768), whole(768, DB)]
        + SUMS + [own_cot] + [whole(512, DB)] * 3,
        [turned_rows(DB), turned_rows(DB), turned_rows(768), turned_rows(1536), turned_rows(DB), whole(8, 512)]
        + [whole(512, DB)] * 4,
        [bf(2048, DB), bf(2048, DB), bf(2048, 768), bf(2048, 1536), f32(2048, DB), f32(8, 512)]
        + [bf(512, DB)] * 4,
        (7_300_000_000, 24_000_000),
    )(at, resid, gain, wg, wu, wd, *squares, grad_out, *cots)
    inners = around(inner, "x")
    g_resid, g_second = call(
        resid_grad_kernel, (4,),
        [rows(DB), rows(DB), whole(1, DB), rows(DB), rows(DB), rows(DB)] + SUMS + SUMS,
        [rows(DB), PIECES],
        [bf(2048, DB), bf(32, 8, 8, DB)],
        (50_000_000, 12_000_000),
    )(at, resid, cot, gain, g_normed, input_mlp, pgate, *squares, *inners)
    g_second, normed, hidden, grads, cot, mixed, inners = lax.optimization_barrier(
        (g_second, normed, hidden, grads, cot, mixed, inners)
    )
    piece = lax.all_to_all(g_second, PLANE, split_axis=0, concat_axis=0, tiled=True)

    mixed = send_each(mixed, "x")
    mixed_out = call(
        mixed_join_kernel, (1,), [whole(512, DB)] * 4, whole(512, D),
        bf(512, D), (1, 1),
    )(at, *mixed)
    g_direct, term_entry = call(
        direct_kernel, (4,),
        [rows(DB), rows(DB), PIECES, rows(DB), whole(DB, DB)],
        [columns(DB), whole(DB, DB)],
        [bf(DB, 2048), f32(DB, DB)],
        (1, 1),
    )(at, g_resid, input_mlp, second, pgate, win)

    halves = whole(32, 6, 8, DB)
    keep, give = call(
        weight_grad_kernel, (2,),
        [rows(DB, 1024), rows(1536, 1024), rows(768, 1024), rows(DB, 1024), whole(DB, DB)] + SUMS,
        [halves] * 2, [bf(32, 6, 8, DB)] * 2, (1, 1),
        [pltpu.VMEM((DB, 1536), F32), pltpu.VMEM((768, DB), F32)],
    )(at, normed, grads, hidden, cot, term_entry, *inners)
    got = lax.ppermute(give, "core", SWAP)

    first_grad, second_grad = call(
        first_grad_kernel, (1,),
        [all_pieces, whole(8, 256, 256), halves, halves],
        [whole(32, 14, 8, DB), whole(8, 256, DB)],
        [bf(32, 14, 8, DB), bf(8, 256, DB)],
        (400_000_000, 6_000_000), wide,
    )(at, piece, f2, keep, got)
    square_scratch = [pltpu.VMEM((256, 256), F32)]
    term_out = pl.BlockSpec((2, 64, 256), lambda t, s: (t, 0, 0))

    first_grad, second_grad = lax.optimization_barrier((first_grad, second_grad))
    g_first = lax.all_to_all(first_grad, PLANE, split_axis=0, concat_axis=0, tiled=True)

    def factor_sums(terms):
        return call(
            factor_sum_kernel, (1,), [whole(8, 64, 256)] * 4, [whole(8, 32, 256)] * 2,
            [f32(8, 32, 256), bf(8, 32, 256)], (1, 1),
        )(at, *terms)

    def factor_gradient(own, got, slots):
        shape = (slots, 8 // slots, 32, 256)
        joined = call(
            factor_join_kernel, (1,), [whole(*shape)] * 2, whole(slots, 2, 8 // slots, 32, 256),
            f32(slots, 2, 8 // slots, 32, 256), (1, 1),
        )(at, own.reshape(shape), got.reshape(shape))
        return joined.reshape(16, 32, 256)

    terms_two = call(
        term_two_kernel, (4,),
        [pl.BlockSpec((2, 256, DB), lambda t, s: (t, 0, 0))] * 2,
        [term_out] * 4, [bf(8, 64, 256)] * 4, (1, 1), square_scratch,
    )(at, second_grad, first_cols)
    sums_two = factor_sums(send_each(terms_two, "x"))

    g_first, sums_two, mixed_out = lax.optimization_barrier((g_first, sums_two, mixed_out))
    own_grad, give_grad = call(
        back_kernel, (4,),
        [PIECES, pl.BlockSpec((1, 2, 256, 256), lambda t, s: (2 * t + s[0], 0, 0, 0)), columns(DB)],
        [columns(192), columns(192)],
        [bf(192, 2048), bf(192, 2048)],
        (12_000_000_000, 6_000_000),
    )(at, g_first, factor_one.reshape(8, 2, 256, 256), g_direct)
    got_two = lax.ppermute(sums_two[1], "zh", SWAP)
    g_first, give_grad, got_two = lax.optimization_barrier((g_first, give_grad, got_two))
    terms_one = call(
        term_one_kernel, (4,), [PIECES, rows(DB)],
        [term_out] * 4, [bf(8, 64, 256)] * 4, (1, 1), square_scratch,
    )(at, g_first, input_mlp)

    got_two, terms_one = lax.optimization_barrier((got_two, terms_one))
    for_sums, terms_one = lax.optimization_barrier((g_first, terms_one))
    terms_one = send_each(terms_one, "x")
    got_grad = lax.ppermute(give_grad, "zh", SWAP)
    summed = call(
        weight_sum_kernel, (3,),
        [pl.BlockSpec((32, 2, 8, DB), lambda t, s: (0, t + 4, 0, 0))],
        pl.BlockSpec((2, 2, 8, DB), lambda t, s: (0, t, 0, 0)), f32(2, 6, 8, DB), (1, 1),
    )(at, for_sums)
    back = [(there, here) for here, there in shard_moves()]
    own = lax.ppermute(summed, ALL, back)
    grad_norm_gain = summed[0].reshape(48, DB)[36:40].reshape(D)

    grad_factor_two = factor_gradient(sums_two[0], got_two, 1)
    sums_one = factor_sums(terms_one)
    give_one, got_grad = lax.optimization_barrier((sums_one[1], got_grad))
    got_one = lax.ppermute(give_one, "zh", SWAP)
    own, got_one = lax.optimization_barrier((own, got_one))
    own = own.reshape(2, 48, DB)
    low, high = own[0], own[1]
    grad_w_gate = jnp.concatenate([low[:12], low[12:24]], axis=1)
    grad_w_up = jnp.concatenate([high[:12], high[12:24]], axis=1)
    grad_w_input_gate = low[24:36]
    grad_w_down = high[24:]
    grad_factor_one = factor_gradient(sums_one[0], got_one, 4)
    grad_inputs = call(
        join_kernel, (2,), [columns(192, 1024)] * 2, columns(192, 2048), bf(192, 4096), (1, 1)
    )(at, own_grad, got_grad).T
    return (
        mixed_out,
        grad_inputs,
        grad_factor_one,
        grad_factor_two,
        grad_w_input_gate,
        grad_norm_gain,
        grad_w_gate,
        grad_w_up,
        grad_w_down,
    )


def solution(mesh):
    fine = Mesh(mesh.devices.reshape(SIZES), ALL)
    return jax.shard_map(
        per_device,
        mesh=fine,
        in_specs=(
            P(SEQ, CH),
            P(SEQ, None, None),
            P(SEQ, None, None),
            P(ALL, None),
            P(),
            P(ALL, None),
            P(ALL, None),
            P(ALL, None),
            P(ALL, None),
        ),
        out_specs=(
            P(ALL, None),
            P(SEQ, CH),
            P(SEQ, CH, None),
            P(SEQ, CH, None),
            P(ALL, None),
            P(),
            P(ALL, None),
            P(ALL, None),
            P(ALL, None),
        ),
        check_vma=False,
    )
```

```python
import math

import jax
import jax.numpy as jnp
from jax import lax
from jax.experimental import pallas as pl
from jax.experimental.pallas import tpu as pltpu
from jax.sharding import Mesh
from jax.sharding import PartitionSpec as P

D = 1536
NBLK = 4
SEQL = 65536
DB = D // NBLK
BF = jnp.bfloat16
F32 = jnp.float32

SEQ = ("zl", "y", "core")
CH = ("x", "zh")
ALL = SEQ + CH
SIZES = (2, 4, 2, 4, 2)
PLANE = SEQ + ("zh",)


def index_of(zl, y, k, x, zh):
    return (((zl * 4 + y) * 2 + k) * 4 + x) * 2 + zh


def shard_moves():
    moves = []
    for zl in range(2):
        for y in range(4):
            for k in range(2):
                for x in range(4):
                    for zh in range(2):
                        there = index_of(y % 2, k * 2 + x // 2, x % 2, zl * 2 + y // 2, zh)
                        moves.append((index_of(zl, y, k, x, zh), there))
    return moves


SWAP = [(0, 1), (1, 0)]


def call(body, grid, ins, outs, shapes, cost, scratch=()):
    return pl.pallas_call(
        body,
        grid_spec=pltpu.PrefetchScalarGridSpec(
            num_scalar_prefetch=1,
            grid=grid,
            in_specs=ins,
            out_specs=outs,
            scratch_shapes=list(scratch),
        ),
        out_shape=shapes,
        name=body.__name__,
        compiler_params=pltpu.CompilerParams(
            dimension_semantics=("arbitrary",) * len(grid), vmem_limit_bytes=56 * 1024 * 1024
        ),
        cost_estimate=pl.CostEstimate(flops=cost[0], bytes_accessed=cost[1], transcendentals=0),
    )


def whole(*shape):
    return pl.BlockSpec(shape, lambda t, s: (0,) * len(shape))


def rows(width, height=512):
    return pl.BlockSpec((height, width), lambda t, s: (t, 0))


def turned_rows(width, height=512):
    return pl.BlockSpec((height, width), lambda t, s: (lax.rem(s[1] + t, 4), 0))


def columns(height, width=512):
    return pl.BlockSpec((height, width), lambda t, s: (0, t))


PIECES = pl.BlockSpec((32, 2, 8, DB), lambda t, s: (0, t, 0, 0))
PAIRS = pl.BlockSpec((32, 4, 8, DB), lambda t, s: (0, t, 0, 0))
SUMS = [whole(8, 512)] * 4


def read_pieces(ref):
    return jnp.concatenate(
        [ref[:, r].astype(F32).reshape(256, DB) for r in range(2)], axis=0
    )


def row_sums(value):
    ones = jnp.ones((8, DB), BF)
    high = value.astype(BF)
    low = (value - high.astype(F32)).astype(BF)
    return dot_t(ones, high) + dot_t(ones, low)


def row_of(refs, at):
    total = refs[0][...] + refs[1][...] + refs[2][...] + refs[3][...]
    here = lax.broadcasted_iota(jnp.int32, (8, 512), 0) == at
    return jnp.sum(jnp.where(here, total, 0.0), axis=0, keepdims=True)


def put_row(ref, at, value):
    here = lax.broadcasted_iota(jnp.int32, (8, 512), 0) == at
    ref[...] = jnp.where(here, value, ref[...])


def as_column(row):
    turned = jnp.transpose(jnp.broadcast_to(row, (128, row.shape[1])))
    return jnp.concatenate([turned] * (DB // 128), axis=1)


def dot(a, b):
    return jnp.dot(a, b, preferred_element_type=F32)


def dot_t(a, b):
    return lax.dot_general(a, b, (((1,), (1,)), ((), ())), preferred_element_type=F32)


def t_dot(a, b):
    return lax.dot_general(a, b, (((0,), (0,)), ((), ())), preferred_element_type=F32)


def sigmoid(value):
    return 0.5 * jnp.tanh(0.5 * value) + 0.5


def first_kernel(_, f1_ref, in_ref, payload_ref, out_ref):
    step = pl.program_id(0)

    @pl.when(step < 4)
    def _():
        for q in range(2):
            results = []
            for r in range(2 * q, 2 * q + 2):
                value = dot_t(f1_ref[r], in_ref[:, r * 256 : (r + 1) * 256])
                results.append(value.reshape(32, 8, 192))
            out_ref[:, q] = jnp.concatenate(results, axis=2).astype(BF)

    @pl.when(step >= 4)
    def _():
        for q in range(2):
            slot = lax.max(2 * step - 8, 0) + q
            halves = [payload_ref[core, slot] for core in range(2)]
            for dev in range(32):
                out_ref[dev, q] = halves[dev // 2 % 2]


def copy_kernel(_, in_ref, out_ref):
    out_ref[...] = in_ref[...]


def copy_three_kernel(_, *refs):
    for j in range(3):
        refs[3 + j][...] = refs[j][...]


def put_rows(refs, row, value):
    for j, ref in enumerate(refs):
        ref[row : row + value.shape[0], :] = value[:, j * 128 : (j + 1) * 128]


def put_position(refs, a, value):
    for j, ref in enumerate(refs):
        ref[pl.ds(a, 256, stride=8), :] = value[:, j * 128 : (j + 1) * 128]


def take_position(refs, a):
    parts = [ref[pl.ds(a, 256, stride=8), :] for ref in refs]
    return jnp.concatenate(parts, axis=1).astype(BF)


def second_kernel(_, piece_ref, f2_ref, out_ref, first_ref, *scratch):
    cols, result = scratch[:3], scratch[3:]
    for s in range(16):
        for pair in range(8):
            low, high = (piece_ref[2 * s + h, pair].astype(F32) for h in range(2))
            row = (s * 16 + pair * 2) * 8
            put_rows(cols, row, jnp.concatenate([low[:, :192], high[:, :192]], axis=1))
            put_rows(cols, row + 8, jnp.concatenate([low[:, 192:], high[:, 192:]], axis=1))
    for a in range(8):
        first = take_position(cols, a)
        first_ref[a] = first
        put_position(result, a, dot(f2_ref[a], first))
    write_blocks(result, out_ref)


def first_grad_kernel(_, piece_ref, f2_ref, keep_ref, got_ref, out_ref, grad_ref, *scratch):
    cols, result = scratch[:3], scratch[3:]
    for dev in range(32):
        s, h = dev // 2, dev % 2
        for x in range(4):
            row = (s * 16 + x * 4 + h * 2) * 8
            put_rows(cols, row, piece_ref[dev, 2 * x : 2 * x + 2].astype(F32).reshape(16, DB))
    for a in range(8):
        grad = take_position(cols, a)
        grad_ref[a] = grad
        put_position(result, a, t_dot(f2_ref[a], grad))
    write_blocks(result, out_ref)
    for dev in range(32):
        total = keep_ref[dev].astype(F32) + got_ref[dev].astype(F32)
        out_ref[dev, 8:] = total.astype(BF)


def write_blocks(result, out_ref):
    for dev in range(32):
        s, h = dev // 2, dev % 2
        for x in range(4):
            row = (s * 16 + x * 4 + h * 2) * 8
            value = jnp.concatenate([ref[row : row + 16, :] for ref in result], axis=1)
            out_ref[dev, 2 * x : 2 * x + 2] = value.reshape(2, 8, DB).astype(BF)


def gating_kernel(s_ref, own_ref, got_ref, second_ref, win_ref, in_ref, resid_ref, pgate_ref, sum_ref):
    zh = s_ref[0]
    own, got = own_ref[...], got_ref[...]
    first_half = jnp.where(zh == 0, own, got)
    second_half = jnp.where(zh == 0, got, own)
    value = jnp.transpose(jnp.concatenate([first_half, second_half], axis=0))
    in_ref[...] = value
    pgate = dot(value, win_ref[...]).astype(BF)
    pgate_ref[...] = pgate
    value_f = value.astype(F32)
    silu_in = value_f * sigmoid(value_f)
    resid = (value_f + read_pieces(second_ref) * pgate.astype(F32) * silu_in).astype(BF)
    resid_ref[...] = resid
    resid_f = resid.astype(F32)

    @pl.when(pl.program_id(0) == 0)
    def _():
        sum_ref[...] = jnp.zeros_like(sum_ref)

    put_row(sum_ref, pl.program_id(0), row_sums(resid_f * resid_f))


def mlp_kernel(s_ref, resid_ref, gain_ref, wg_ref, wu_ref, wd_ref, *refs):
    squares, cots = refs[:4], refs[4:8]
    cot_ref, normed_ref, hidden_ref, grads_ref, gnormed_ref, inner_ref = refs[8:14]
    mixed_refs = refs[14:18]
    step = pl.program_id(0)
    chunk = lax.rem(s_ref[1] + step, 4)
    for j in range(4):

        @pl.when(step == j)
        def _(j=j):
            cot_ref[...] = cots[j][...]

    cot = cot_ref[...]
    resid_f = resid_ref[...].astype(F32)
    rstd = as_column(lax.rsqrt(row_of(squares, chunk) * (1.0 / D) + 1e-06))
    gain = gain_ref[...]
    scaled_resid = resid_f * rstd
    normed = (scaled_resid * gain).astype(BF)
    normed_ref[...] = normed
    gate = dot(normed, wg_ref[...])
    upper = dot(normed, wu_ref[...])
    g_hidden = dot_t(cot, wd_ref[...])
    sig = sigmoid(gate)
    act = gate * sig
    hidden = (act * upper).astype(BF)
    hidden_ref[...] = hidden
    g_gate = (g_hidden * upper * (sig + act * (1.0 - sig))).astype(BF)
    g_up = (g_hidden * act).astype(BF)
    grads_ref[:, :768] = g_gate
    grads_ref[:, 768:] = g_up
    mixed = (resid_f + dot(hidden, wd_ref[...])).astype(BF)
    for j in range(4):

        @pl.when(step == j)
        def _(j=j):
            mixed_refs[j][...] = mixed

    g_normed = dot_t(g_gate, wg_ref[...]) + dot_t(g_up, wu_ref[...])
    gnormed_ref[...] = g_normed

    @pl.when(step == 0)
    def _():
        inner_ref[...] = jnp.zeros_like(inner_ref)

    put_row(inner_ref, chunk, row_sums(g_normed * gain * resid_f))
    inner_ref[4:5, :DB] += jnp.sum(g_normed * scaled_resid, axis=0, keepdims=True)


def resid_grad_kernel(
    _, resid_ref, cot_ref, gain_ref, gnormed_ref, in_ref, pgate_ref, *refs
):
    squares, inners, (g_resid_ref, g_second_ref) = refs[:4], refs[4:8], refs[8:]
    for q in range(2):
        chunk = 2 * pl.program_id(0) + q
        here = slice(q * 512, (q + 1) * 512)
        rstd_row = lax.rsqrt(row_of(squares, chunk) * (1.0 / D) + 1e-06)
        rstd = as_column(rstd_row)
        factor = as_column(rstd_row * rstd_row * rstd_row * (row_of(inners, chunk) * (1.0 / D)))
        scaled = gnormed_ref[here] * gain_ref[...]
        g_resid = (
            cot_ref[here].astype(F32) + rstd * scaled - resid_ref[here].astype(F32) * factor
        ).astype(BF)
        g_resid_ref[here] = g_resid
        value = in_ref[here].astype(F32)
        silu_in = value * sigmoid(value)
        g_second = (g_resid.astype(F32) * pgate_ref[here].astype(F32) * silu_in).astype(BF)
        for r in range(2):
            g_second_ref[:, 2 * q + r] = g_second[r * 256 : (r + 1) * 256].reshape(32, 8, DB)


def direct_kernel(_, g_resid_ref, in_ref, second_ref, pgate_ref, win_ref, g_direct_ref, term_ref):
    resid_grad = g_resid_ref[...].astype(F32)
    value = in_ref[...].astype(F32)
    sig = sigmoid(value)
    second = read_pieces(second_ref)
    g_pgate = (resid_grad * second * (value * sig)).astype(BF)
    slope = sig * (1.0 + value * (1.0 - sig))
    through = dot_t(g_pgate, win_ref[...])
    g_direct_ref[...] = jnp.transpose(
        (resid_grad * (1.0 + second * pgate_ref[...].astype(F32) * slope) + through).astype(BF)
    )
    term = t_dot(in_ref[...], g_pgate)

    @pl.when(pl.program_id(0) == 0)
    def _():
        term_ref[...] = jnp.zeros_like(term_ref)

    term_ref[...] += term


def put_terms(s_ref, term, scratch, refs, slot):
    scratch[...] = term * (1.0 / math.sqrt(D))
    for j in range(4):
        start = pl.multiple_of(lax.rem(s_ref[1] + j, 4) * 64, 64)
        refs[j][slot] = scratch[pl.ds(start, 64), :].astype(BF)


def term_two_kernel(s_ref, grad_ref, first_ref, *refs):
    for a in range(2):
        put_terms(s_ref, dot_t(grad_ref[a], first_ref[a]), refs[4], refs[:4], a)


def term_one_kernel(s_ref, g_first_ref, in_ref, *refs):
    for r in range(4):
        g_first = g_first_ref[:, r].reshape(256, DB)
        term = dot_t(g_first, in_ref[r * 256 : (r + 1) * 256])
        put_terms(s_ref, term, refs[4], refs[:4], r)


def factor_sum_kernel(s_ref, a_ref, b_ref, c_ref, d_ref, own_ref, give_ref):
    zh = s_ref[0]
    total = (
        a_ref[...].astype(F32) + b_ref[...].astype(F32)
        + c_ref[...].astype(F32) + d_ref[...].astype(F32)
    )
    low, high = total[:, :32], total[:, 32:]
    own_ref[...] = jnp.where(zh == 0, low, high)
    give_ref[...] = jnp.where(zh == 0, high, low).astype(BF)


def factor_join_kernel(s_ref, own_ref, got_ref, out_ref):
    zh = s_ref[0]
    own, got = own_ref[...], got_ref[...].astype(F32)
    out_ref[:, 0] = jnp.where(zh == 0, own, got)
    out_ref[:, 1] = jnp.where(zh == 0, got, own)


def back_kernel(s_ref, g_first_ref, f1_ref, direct_ref, own_ref, give_ref):
    zh = s_ref[0]
    for r in range(4):
        here = slice(r * 256, (r + 1) * 256)
        back = t_dot(g_first_ref[:, r].reshape(256, DB), f1_ref[r // 2, 0, r % 2])
        total = direct_ref[:, here].astype(F32) + back
        low, high = total[:192], total[192:]
        own_ref[:, here] = jnp.where(zh == 0, low, high).astype(BF)
        give_ref[:, here] = jnp.where(zh == 0, high, low).astype(BF)


def join_kernel(s_ref, own_ref, got_ref, out_ref):
    zh = s_ref[0]
    for q in range(2):
        here = slice(q * 512, (q + 1) * 512)
        own, got = own_ref[:, here], got_ref[:, here]
        out_ref[:, q * 1024 : q * 1024 + 512] = jnp.where(zh == 0, own, got)
        out_ref[:, q * 1024 + 512 : (q + 1) * 1024] = jnp.where(zh == 0, got, own)


def mixed_join_kernel(s_ref, *refs):
    for j in range(4):
        start = pl.multiple_of(lax.rem(s_ref[1] + 4 - j, 4) * DB, DB)
        refs[4][:, pl.ds(start, DB)] = refs[j][...]


def payload_kernel(_, wg_ref, wu_ref, win_ref, wd_ref, out_ref):
    wg, wu = wg_ref[...].astype(F32), wu_ref[...].astype(F32)
    win, down = win_ref[...].astype(F32), wd_ref[...].astype(F32)
    put_half(out_ref, 0, [wg[:, :DB], wg[:, DB:], win, jnp.zeros_like(win)])
    put_half(out_ref, 1, [wu[:, :DB], wu[:, DB:], down])


def put_half(ref, at, parts):
    ref[at] = jnp.concatenate(parts, axis=0).reshape(6, 8, DB).astype(BF)


def gather_kernel(_, *refs):
    for j in range(4):
        refs[4][:, j * 512 : (j + 1) * 512] = refs[j][...]


def weights_kernel(s_ref, own_ref, across_ref, wg_ref, wu_ref, win_ref, wd_ref):
    first = s_ref[4] == 0
    gates, ups, entries, downs = [], [], [], []
    for shard in range(8):
        own = own_ref[shard].astype(F32).reshape(48, DB)
        across = across_ref[shard].astype(F32).reshape(48, DB)
        low, high = jnp.where(first, own, across), jnp.where(first, across, own)
        gates.append(jnp.concatenate([low[:12], low[12:24]], axis=1))
        entries.append(low[24:36])
        ups.append(jnp.concatenate([high[:12], high[12:24]], axis=1))
        downs.append(high[24:])
    for ref, parts in ((wg_ref, gates), (wu_ref, ups), (win_ref, entries), (wd_ref, downs)):
        ref[...] = jnp.concatenate(parts, axis=0).astype(BF)


def weight_grad_kernel(
    s_ref, normed_ref, grads_ref, hidden_ref, cot_ref, entry_ref, *refs,
):
    inners, (keep_ref, give_ref, across, down) = refs[:4], refs[4:]
    step = pl.program_id(0)

    @pl.when(step == 0)
    def _():
        across[...] = jnp.zeros_like(across)
        down[...] = jnp.zeros_like(down)

    across[...] += t_dot(normed_ref[...], grads_ref[...])
    down[...] += t_dot(hidden_ref[...], cot_ref[...])

    @pl.when(step == pl.num_programs(0) - 1)
    def _():
        first = s_ref[4] == 0
        fill = jnp.zeros((8, DB), F32)
        block = lax.broadcasted_iota(jnp.int32, (4, DB), 0)
        gains = jnp.zeros((4, DB), F32)
        for j in range(4):
            mine = jnp.broadcast_to(inners[j][4:5, :DB], (4, DB))
            gains = gains + jnp.where(block == lax.rem(s_ref[1] + j, 4), mine, 0.0)
        for shard in range(32):
            here = slice(shard * 12, shard * 12 + 12)
            gates, entries = across[here, :], entry_ref[here, :]
            low = [gates[:, :DB], gates[:, DB : 2 * DB], entries, gains, fill]
            high = [gates[:, 2 * DB : 3 * DB], gates[:, 3 * DB :]]
            high.append(down[shard * 24 : shard * 24 + 24, :])
            low = jnp.concatenate(low, axis=0)
            high = jnp.concatenate(high, axis=0)
            put_half(keep_ref, shard, [jnp.where(first, low, high)])
            put_half(give_ref, shard, [jnp.where(first, high, low)])


def weight_sum_kernel(_, in_ref, out_ref):
    for core in range(2):
        total = jnp.zeros((2, 8, DB), F32)
        for pair in range(8):
            for zh in range(2):
                total = total + in_ref[pair * 4 + core * 2 + zh].astype(F32)
        out_ref[core] = total * (1.0 / math.sqrt(SEQL))


def turn(axis, size, step):
    return [(i, (i + step) % size) for i in range(size)]


def around(value, axis):
    return [value] + [lax.ppermute(value, axis, turn(axis, 4, -j)) for j in (1, 2, 3)]


def send_each(parts, axis):
    return [parts[0]] + [lax.ppermute(parts[j], axis, turn(axis, 4, j)) for j in (1, 2, 3)]


Z_RING = ("zl", "zh")


def per_device(
    inputs, factor_one, factor_two, w_input_gate, norm_gain, w_gate, w_up, w_down, grad_out
):
    tok_scale = 1.0 / math.sqrt(SEQL)
    zh = lax.axis_index("zh")
    xi = lax.axis_index("x")
    yi = lax.axis_index("y")
    core = lax.axis_index("core")
    zi = lax.axis_index("zl") * 2 + zh
    at = jnp.stack([zh, xi, yi, zi, core]).astype(jnp.int32)
    bf = lambda *shape: jax.ShapeDtypeStruct(shape, BF)
    f32 = lambda *shape: jax.ShapeDtypeStruct(shape, F32)
    turned_in = inputs.T

    give = call(
        gather_kernel, (1,),
        [pl.BlockSpec((192, 512), lambda t, s, q=q: (0, 2 * q + 1 - s[0])) for q in range(4)],
        whole(192, 2048), bf(192, 2048), (1, 1),
    )(at, *[turned_in] * 4)
    other = lax.ppermute(give, "zh", SWAP)
    give, turned_in, w_gate = lax.optimization_barrier((give, turned_in, w_gate))

    payload = call(
        payload_kernel, (1,),
        [whole(12, 768), whole(12, 768), whole(12, DB), whole(24, DB)],
        whole(2, 6, 8, DB), bf(2, 6, 8, DB), (1, 1),
    )(at, w_gate, w_up, w_input_gate, w_down)
    payload = lax.ppermute(payload, ALL, shard_moves())
    first_local = call(
        first_kernel, (7,),
        [pl.BlockSpec((4, 256, 256), lambda t, s: (lax.min(t, 3), 0, 0)),
         pl.BlockSpec((192, 1024), lambda t, s: (0, lax.min(t, 3))), whole(2, 6, 8, DB)],
        pl.BlockSpec((32, 2, 8, DB), lambda t, s: (0, t, 0, 0)),
        bf(32, 14, 8, DB),
        (1, 1),
    )(at, factor_one, turned_in, payload)
    first_local, other, turned_in, grad_out, factor_two = lax.optimization_barrier(
        (first_local, other, turned_in, grad_out, factor_two)
    )
    piece = lax.all_to_all(first_local, PLANE, split_axis=0, concat_axis=0, tiled=True)
    gain = lax.dynamic_slice_in_dim(norm_gain, xi * DB, DB, 0).reshape(1, DB)

    to_send = call(
        copy_three_kernel, (1,),
        [pl.BlockSpec((512, DB), lambda t, s, j=j: (0, lax.rem(s[1] + 4 - j, 4))) for j in (1, 2, 3)],
        [whole(512, DB)] * 3, [bf(512, DB)] * 3, (1, 1),
    )(at, grad_out, grad_out, grad_out)
    cots = [lax.ppermute(to_send[j - 1], "x", turn("x", 4, -j)) for j in (1, 2, 3)]
    f2 = lax.dynamic_slice_in_dim(factor_two, zh * 8, 8, 0)

    wide = [pltpu.VMEM((2048, 128), F32)] * 6
    all_pieces = whole(32, 8, 8, DB)
    second_cols, first_cols = call(
        second_kernel, (1,),
        [whole(32, 14, 8, DB), whole(8, 256, 256)],
        [all_pieces, whole(8, 256, DB)],
        [bf(32, 8, 8, DB), bf(8, 256, DB)],
        (400_000_000, 6_000_000), wide,
    )(at, piece, f2)
    second_cols, piece = lax.optimization_barrier((second_cols, piece))
    second = lax.all_to_all(second_cols, PLANE, split_axis=0, concat_axis=0, tiled=True)

    half = piece[:, 8:]
    across = lax.ppermute(half, "core", SWAP)
    shards = pl.BlockSpec((8, 6, 8, DB), lambda t, s: (t, 0, 0, 0))
    wg, wu, win, wd = call(
        weights_kernel, (4,), [shards] * 2,
        [rows(768, 96), rows(768, 96), rows(DB, 96), rows(DB, 192)],
        [bf(DB, 768), bf(DB, 768), bf(DB, DB), bf(768, DB)], (1, 1),
    )(at, half, across)

    input_mlp, resid, pgate, square = call(
        gating_kernel, (4,),
        [pl.BlockSpec((192, 512), lambda t, s: (0, 2 * t + s[0])),
         columns(192), PIECES, whole(DB, DB)],
        [rows(DB), rows(DB), rows(DB), whole(8, 512)],
        [bf(2048, DB), bf(2048, DB), bf(2048, DB), f32(8, 512)],
        (600_000_000, 10_000_000),
    )(at, turned_in, other, second, win)
    squares = around(square, "x")
    own_cot = pl.BlockSpec((512, DB), lambda t, s: (0, s[1]))
    cot, normed, hidden, grads, g_normed, inner, *mixed = call(
        mlp_kernel, (4,),
        [turned_rows(DB), whole(1, DB), whole(DB, 768), whole(DB, 768), whole(768, DB)]
        + SUMS + [own_cot] + [whole(512, DB)] * 3,
        [turned_rows(DB), turned_rows(DB), turned_rows(768), turned_rows(1536), turned_rows(DB), whole(8, 512)]
        + [whole(512, DB)] * 4,
        [bf(2048, DB), bf(2048, DB), bf(2048, 768), bf(2048, 1536), f32(2048, DB), f32(8, 512)]
        + [bf(512, DB)] * 4,
        (7_300_000_000, 24_000_000),
    )(at, resid, gain, wg, wu, wd, *squares, grad_out, *cots)
    inners = around(inner, "x")
    g_resid, g_second = call(
        resid_grad_kernel, (2,),
        [rows(DB, 1024)] * 2 + [whole(1, DB)] + [rows(DB, 1024)] * 3 + SUMS + SUMS,
        [rows(DB, 1024), PAIRS],
        [bf(2048, DB), bf(32, 8, 8, DB)],
        (50_000_000, 12_000_000),
    )(at, resid, cot, gain, g_normed, input_mlp, pgate, *squares, *inners)
    g_second, normed, hidden, grads, cot, mixed, inners = lax.optimization_barrier(
        (g_second, normed, hidden, grads, cot, mixed, inners)
    )
    piece = lax.all_to_all(g_second, PLANE, split_axis=0, concat_axis=0, tiled=True)

    mixed = send_each(mixed, "x")
    mixed_out = call(
        mixed_join_kernel, (1,), [whole(512, DB)] * 4, whole(512, D),
        bf(512, D), (1, 1),
    )(at, *mixed)
    g_direct, term_entry = call(
        direct_kernel, (4,),
        [rows(DB), rows(DB), PIECES, rows(DB), whole(DB, DB)],
        [columns(DB), whole(DB, DB)],
        [bf(DB, 2048), f32(DB, DB)],
        (1, 1),
    )(at, g_resid, input_mlp, second, pgate, win)

    halves = whole(32, 6, 8, DB)
    keep, give = call(
        weight_grad_kernel, (2,),
        [rows(DB, 1024), rows(1536, 1024), rows(768, 1024), rows(DB, 1024), whole(DB, DB)] + SUMS,
        [halves] * 2, [bf(32, 6, 8, DB)] * 2, (1, 1),
        [pltpu.VMEM((DB, 1536), F32), pltpu.VMEM((768, DB), F32)],
    )(at, normed, grads, hidden, cot, term_entry, *inners)
    got = lax.ppermute(give, "core", SWAP)

    first_grad, second_grad = call(
        first_grad_kernel, (1,),
        [all_pieces, whole(8, 256, 256), halves, halves],
        [whole(32, 14, 8, DB), whole(8, 256, DB)],
        [bf(32, 14, 8, DB), bf(8, 256, DB)],
        (400_000_000, 6_000_000), wide,
    )(at, piece, f2, keep, got)
    square_scratch = [pltpu.VMEM((256, 256), F32)]
    term_out = pl.BlockSpec((2, 64, 256), lambda t, s: (t, 0, 0))

    first_grad, second_grad = lax.optimization_barrier((first_grad, second_grad))
    g_first = lax.all_to_all(first_grad, PLANE, split_axis=0, concat_axis=0, tiled=True)

    def factor_sums(terms):
        return call(
            factor_sum_kernel, (1,), [whole(8, 64, 256)] * 4, [whole(8, 32, 256)] * 2,
            [f32(8, 32, 256), bf(8, 32, 256)], (1, 1),
        )(at, *terms)

    def factor_gradient(own, got, slots):
        shape = (slots, 8 // slots, 32, 256)
        joined = call(
            factor_join_kernel, (1,), [whole(*shape)] * 2, whole(slots, 2, 8 // slots, 32, 256),
            f32(slots, 2, 8 // slots, 32, 256), (1, 1),
        )(at, own.reshape(shape), got.reshape(shape))
        return joined.reshape(16, 32, 256)

    terms_two = call(
        term_two_kernel, (4,),
        [pl.BlockSpec((2, 256, DB), lambda t, s: (t, 0, 0))] * 2,
        [term_out] * 4, [bf(8, 64, 256)] * 4, (1, 1), square_scratch,
    )(at, second_grad, first_cols)
    sums_two = factor_sums(send_each(terms_two, "x"))

    g_first, sums_two, mixed_out = lax.optimization_barrier((g_first, sums_two, mixed_out))
    own_grad, give_grad = call(
        back_kernel, (2,),
        [PAIRS, pl.BlockSpec((2, 1, 2, 256, 256), lambda t, s: (t, s[0], 0, 0, 0)), columns(DB, 1024)],
        [columns(192, 1024), columns(192, 1024)],
        [bf(192, 2048), bf(192, 2048)],
        (12_000_000_000, 6_000_000),
    )(at, g_first, factor_one.reshape(4, 2, 2, 256, 256), g_direct)
    got_two = lax.ppermute(sums_two[1], "zh", SWAP)
    g_first, give_grad, got_two = lax.optimization_barrier((g_first, give_grad, got_two))
    terms_one = call(
        term_one_kernel, (2,), [PAIRS, rows(DB, 1024)],
        [pl.BlockSpec((4, 64, 256), lambda t, s: (t, 0, 0))] * 4, [bf(8, 64, 256)] * 4, (1, 1), square_scratch,
    )(at, g_first, input_mlp)

    got_two, terms_one = lax.optimization_barrier((got_two, terms_one))
    for_sums, terms_one = lax.optimization_barrier((g_first, terms_one))
    terms_one = send_each(terms_one, "x")
    got_grad = lax.ppermute(give_grad, "zh", SWAP)
    summed = call(
        weight_sum_kernel, (3,),
        [pl.BlockSpec((32, 2, 8, DB), lambda t, s: (0, t + 4, 0, 0))],
        pl.BlockSpec((2, 2, 8, DB), lambda t, s: (0, t, 0, 0)), f32(2, 6, 8, DB), (1, 1),
    )(at, for_sums)
    back = [(there, here) for here, there in shard_moves()]
    own = lax.ppermute(summed, ALL, back)
    grad_norm_gain = summed[0].reshape(48, DB)[36:40].reshape(D)

    grad_factor_two = factor_gradient(sums_two[0], got_two, 1)
    sums_one = factor_sums(terms_one)
    give_one, got_grad = lax.optimization_barrier((sums_one[1], got_grad))
    got_one = lax.ppermute(give_one, "zh", SWAP)
    own, got_one = lax.optimization_barrier((own, got_one))
    own = own.reshape(2, 48, DB)
    low, high = own[0], own[1]
    grad_w_gate = jnp.concatenate([low[:12], low[12:24]], axis=1)
    grad_w_up = jnp.concatenate([high[:12], high[12:24]], axis=1)
    grad_w_input_gate = low[24:36]
    grad_w_down = high[24:]
    grad_factor_one = factor_gradient(sums_one[0], got_one, 4)
    grad_inputs = call(
        join_kernel, (2,), [columns(192, 1024)] * 2, columns(192, 2048), bf(192, 4096), (1, 1)
    )(at, own_grad, got_grad).T
    return (
        mixed_out,
        grad_inputs,
        grad_factor_one,
        grad_factor_two,
        grad_w_input_gate,
        grad_norm_gain,
        grad_w_gate,
        grad_w_up,
        grad_w_down,
    )


def solution(mesh):
    fine = Mesh(mesh.devices.reshape(SIZES), ALL)
    return jax.shard_map(
        per_device,
        mesh=fine,
        in_specs=(
            P(SEQ, CH),
            P(SEQ, None, None),
            P(SEQ, None, None),
            P(ALL, None),
            P(),
            P(ALL, None),
            P(ALL, None),
            P(ALL, None),
            P(ALL, None),
        ),
        out_specs=(
            P(ALL, None),
            P(SEQ, CH),
            P(SEQ, CH, None),
            P(SEQ, CH, None),
            P(ALL, None),
            P(),
            P(ALL, None),
            P(ALL, None),
            P(ALL, None),
        ),
        check_vma=False,
    )
```
